32 devices in a mesh: zg: 4 (over y, core), gx: 8 (over z, x).
Axes of the slice: x: 2, y: 2, z: 4, core: 2. Of those that a mesh axis runs over, the one named last changes fastest.
Arguments:
- observed: float32 [128, 512, 256], P('zg', 'gx'), may hold values from 0.25 to 4
- kernel_x: float32 [33], replicated, may hold values from 0.2 to 1
- kernel_y: float32 [33], replicated, may hold values from 0.2 to 1
- kernel_z: float32 [65], replicated, may hold values from 0.2 to 1
Outputs:
- estimate: float32 [128, 512, 256], P('zg', 'gx')
The draws below stay inside these ranges and needn't reach their ends.
All inputs are finite; a program needn't handle non-finite values.
Results may differ from the reference program's by a relative error of at most 0.0001.
Values sent between devices are 32-bit elements; how exact they have to be, the bound alone decides.
No kernel may reach another device: no remote copies, remote signals or barrier semaphores. Data moves between devices by JAX's collectives and lax.ppermute only.
A program may use at most 64 MiB of HBM per device.

```python
import math
import jax
import jax.numpy as jnp
from jax import lax

KX = 33
KY = 33
KZ = 65
ITERS = 2
Y = 256
Z = 128
X = 512


def level_of(rng, shape, pieces, least, largest):
    gain, own = 1.0, jax.random.fold_in(rng, 6)
    for position, blocks in pieces:
        heights = jnp.exp(jax.random.uniform(jax.random.fold_in(own, position), (blocks,), jnp.float32, least / len(pieces), largest / len(pieces)))
        gain = gain * jnp.repeat(heights, shape[position] // blocks).reshape([-1 if axis == position else 1 for axis in range(len(shape))])
    return gain


def setup_inputs(seed: int = 0) -> dict:
    streams_of = jax.random.split(jax.random.key(seed), 5)
    observed = jnp.clip(jnp.exp(math.log(4.0) - 2.7725887 * jax.random.uniform(streams_of[0], (Z, X, Y), jnp.float32) ** level_of(streams_of[0], (Z, X, Y), ((0, 4), (1, 8)), -0.2, 0.2)), 0.25, 4.0)
    kernel_x = jnp.clip(jnp.exp(jax.random.uniform(streams_of[1], (KX,), jnp.float32, math.log(0.2), math.log(1.0))), 0.2, 1.0)
    kernel_y = jnp.clip(jnp.exp(jax.random.uniform(streams_of[2], (KY,), jnp.float32, math.log(0.2), math.log(1.0))), 0.2, 1.0)
    kernel_z = jnp.clip(jnp.exp(jax.random.uniform(streams_of[3], (KZ,), jnp.float32, math.log(0.2), math.log(1.0))), 0.2, 1.0)
    return dict(observed=observed, kernel_x=kernel_x, kernel_y=kernel_y, kernel_z=kernel_z)


def band(prof, n_out, n_in, offset):
    diff = jnp.arange(n_in, dtype=jnp.int32)[None, :] - jnp.arange(n_out, dtype=jnp.int32)[:, None] + offset

    def add_tap(tap, acc):
        return acc + jnp.where(diff == tap, prof[tap], 0.0)

    return lax.fori_loop(0, prof.shape[0], add_tap, jnp.zeros((n_out, n_in), jnp.float32))


def apply_all(volume, mat_z, mat_x, mat_y):
    hp = lax.Precision.HIGHEST
    out = jnp.einsum('ij,zjy->ziy', mat_x, volume, precision=hp)
    out = jnp.einsum('zxj,ij->zxi', out, mat_y, precision=hp)
    return jnp.einsum('ij,jxy->ixy', mat_z, out, precision=hp)


def reference(observed, kernel_x, kernel_y, kernel_z):
    prof_x = kernel_x / jnp.sum(kernel_x)
    prof_y = kernel_y / jnp.sum(kernel_y)
    prof_z = kernel_z / jnp.sum(kernel_z)
    size_z, size_x, size_y = observed.shape
    half_x = (prof_x.shape[0] - 1) // 2
    half_y = (prof_y.shape[0] - 1) // 2
    half_z = (prof_z.shape[0] - 1) // 2
    fwd_x = band(prof_x, size_x, size_x, half_x)
    fwd_y = band(prof_y, size_y, size_y, half_y)
    fwd_z = band(prof_z, size_z, size_z, half_z)
    adj_x = band(prof_x[::-1], size_x, size_x, half_x)
    adj_y = band(prof_y[::-1], size_y, size_y, half_y)
    adj_z = band(prof_z[::-1], size_z, size_z, half_z)
    estimate = observed
    for step in range(ITERS):
        blurred = apply_all(estimate, fwd_z, fwd_x, fwd_y)
        ratio = observed / blurred
        correction = apply_all(ratio, adj_z, adj_x, adj_y)
        estimate = estimate * correction
    return estimate
```

```python
import functools

import jax
import jax.numpy as jnp
from jax import lax
from jax.experimental import pallas as pl
from jax.experimental.pallas import tpu as pltpu
from jax.sharding import PartitionSpec as P

ITERS = 2
LANES = 128
AXES = ("zg", "gx")
F32 = jnp.float32
BF16 = jnp.bfloat16
VMEM_LIMIT = 40 * 1024 * 1024


def params(n=1):
    return pltpu.CompilerParams(dimension_semantics=("arbitrary",) * n, vmem_limit_bytes=VMEM_LIMIT)


def cost(flops, data):
    return pl.CostEstimate(flops=flops, bytes_accessed=data, transcendentals=0)


def swaps(pairs):
    return [q for a, b in pairs for q in ((a, b), (b, a))]


class Links:
    def __init__(self, n_zg, n_gx):
        chips = n_zg // 2
        dev = lambda z, x: z * n_gx + x
        every = range(n_gx)
        self.inner = swaps((dev(2 * k, x), dev(2 * k + 1, x)) for k in range(chips) for x in every)
        self.x = swaps((dev(2 * k + 1, x), dev(2 * k, x + 1)) for k in range(chips) for x in range(n_gx - 1))
        z_pairs = lambda first: swaps(
            (dev(2 * k + c, x), dev(2 * k + 2 + c, x)) for k in range(first, chips - 1, 2) for c in (0, 1) for x in every
        )
        self.z_even = z_pairs(0)
        self.z_odd = z_pairs(1)


def send(v, pairs):
    return lax.ppermute(v, AXES, pairs)


def split(v):
    hi = v.astype(BF16)
    return hi, (v - hi.astype(F32)).astype(BF16)


def dot(a, b):
    return jnp.dot(a, b, preferred_element_type=F32)


def matrices(ids, kernel_x, kernel_y, kernel_z, slab, group, size_y, n_pieces):
    taps_x, taps_y, taps_z = (k.shape[0] for k in (kernel_x, kernel_y, kernel_z))
    half_x, half_y, half_z = ((n - 1) // 2 for n in (taps_x, taps_y, taps_z))
    m_x, k_x = 2 * group, 4 * group
    m_z, k_z = 2 * slab, n_pieces * slab

    def body(ids_ref, x_ref, y_ref, z_ref, fx_ref, ax_ref, fyh_ref, fyl_ref, ayh_ref, ayl_ref, fz_ref, az_ref):
        core, par = ids_ref[0], ids_ref[1]

        def band(ref, n_taps, diff):
            def step(t, carry):
                fwd, adj, total = carry
                tap = ref[t]
                fwd = jnp.where(diff == t, tap, fwd)
                adj = jnp.where(diff == n_taps - 1 - t, tap, adj)
                return fwd, adj, total + tap

            zero = jnp.zeros(diff.shape, F32)
            fwd, adj, total = lax.fori_loop(0, n_taps, step, (zero, zero, jnp.float32(0.0)))
            return fwd / total, adj / total

        def places(shape, dim, size, bases):
            at = lax.broadcasted_iota(jnp.int32, shape, dim)
            place = at
            for n, base in enumerate(bases):
                place = jnp.where(at // size == n, at - n * size + base, place)
            return place

        e, i = group * core, group * (1 - core)
        outer, inner = -group + 3 * group * core, 2 * group - 3 * group * core
        rows = places((m_x, k_x), 0, group, (e, i))
        cols = places((m_x, k_x), 1, group, (outer, e, i, inner))
        for ref, mat in zip((fx_ref, ax_ref), band(x_ref, taps_x, cols - rows + half_x)):
            hi, lo = split(mat)
            ref[...] = jnp.concatenate([hi, lo, hi], axis=1)

        a, b = slab * (1 - par), slab * par
        even, odd = 2 * slab - 3 * slab * par, -slab + 3 * slab * par
        rows = places((m_z, k_z), 0, slab, (a, b))
        cols = places((m_z, k_z), 1, slab, (a, b, even, odd)[:n_pieces])
        for ref, mat in zip((fz_ref, az_ref), band(z_ref, taps_z, cols - rows + half_z)):
            hi, lo = split(mat)
            ref[...] = jnp.concatenate([hi, lo], axis=0)

        rows_per = 64
        for r in range(0, size_y, rows_per):
            shape = (rows_per, size_y)
            diff = r + lax.broadcasted_iota(jnp.int32, shape, 0) - lax.broadcasted_iota(jnp.int32, shape, 1) + half_y
            mats = band(y_ref, taps_y, diff)
            for hi_ref, lo_ref, mat in zip((fyh_ref, ayh_ref), (fyl_ref, ayl_ref), mats):
                hi_ref[r : r + rows_per, :], lo_ref[r : r + rows_per, :] = split(mat)

    smem = pl.BlockSpec(memory_space=pltpu.SMEM)
    sds = jax.ShapeDtypeStruct
    out = pl.pallas_call(
        body,
        in_specs=[smem] * 4,
        out_shape=[sds((m_x, 3 * k_x), BF16)] * 2 + [sds((size_y, size_y), BF16)] * 4 + [sds((2 * m_z, k_z), BF16)] * 2,
        compiler_params=pltpu.CompilerParams(vmem_limit_bytes=VMEM_LIMIT),
        name="band_matrices",
    )(ids, kernel_x, kernel_y, kernel_z)
    fx, ax, fyh, fyl, ayh, ayl, fz, az = out
    return (fx, (fyh, fyl), fz), (ax, (ayh, ayl), az)


def conv_x(mat, pieces, s, over=None, lane=0, block=8):
    planes, group, lanes = pieces[0].shape
    slab = planes // 2
    steps = slab // block

    def body(m_ref, *refs):
        out_ref = refs[-1]
        m = m_ref[...]
        for z in range(0, block, 2):
            cols = [jnp.concatenate([r[z + n] for r in refs[:4]], axis=0) for n in (0, 1)]
            hi, lo = split(jnp.concatenate(cols, axis=1))
            res = dot(m, jnp.concatenate([hi, hi, lo], axis=0))
            for n in (0, 1):
                v = res[:, n * lanes : (n + 1) * lanes]
                if over is not None:
                    v = refs[4][0, z + n] / v
                out_ref[z + n] = v

    piece = pl.BlockSpec((block, group, lanes), lambda k: (s * steps + k, 0, 0))
    in_specs = [pl.BlockSpec(mat.shape, lambda k: (0, 0))] + [piece] * 4
    args = [mat, *pieces]
    if over is not None:
        in_specs.append(pl.BlockSpec((1, block, 2 * group, lanes), lambda k: (s, k, 0, lane)))
        args.append(over)
    return pl.pallas_call(
        body,
        grid=(steps,),
        in_specs=in_specs,
        out_specs=pl.BlockSpec((block, 2 * group, lanes), lambda k: (k, 0, 0)),
        out_shape=jax.ShapeDtypeStruct((slab, 2 * group, lanes), F32),
        cost_estimate=cost(2 * slab * lanes * mat.size, 4 * 6 * slab * group * lanes),
        compiler_params=params(),
        name="conv_x",
    )(*args)


def conv_z(mat, pieces, g, over=None, lane=0, block=8):
    slab, width, lanes = pieces[0].shape
    group = width // 2
    steps = group // block
    n = len(pieces)
    m_z = 2 * slab

    def body(m_ref, *refs):
        out = refs[-1].reshape(m_z * block, lanes)
        m = m_ref[...]
        flat = [r.reshape(slab * block, lanes) for r in refs[:n]]
        for x in range(0, block, 2):
            cols = [
                jnp.concatenate([r[pl.ds(x + j, slab, stride=block), :] for r in flat], axis=0) for j in (0, 1)
            ]
            hi, lo = split(jnp.concatenate(cols, axis=1))
            both = dot(m, hi)
            res = both[:m_z] + (both[m_z:] + dot(m[:m_z], lo))
            for j in (0, 1):
                v = res[:, j * lanes : (j + 1) * lanes]
                if over is not None:
                    v = refs[n].reshape(m_z * block, lanes)[pl.ds(x + j, m_z, stride=block), :] / v
                out[pl.ds(x + j, m_z, stride=block), :] = v

    piece = pl.BlockSpec((slab, block, lanes), lambda k: (0, g * steps + k, 0))
    in_specs = [pl.BlockSpec(mat.shape, lambda k: (0, 0))] + [piece] * n
    args = [mat, *pieces]
    if over is not None:
        in_specs.append(pl.BlockSpec((2, slab, block, lanes), lambda k: (0, 0, g * steps + k, lane)))
        args.append(over)
    return pl.pallas_call(
        body,
        grid=(steps,),
        in_specs=in_specs,
        out_specs=pl.BlockSpec((m_z, block, lanes), lambda k: (0, k, 0)),
        out_shape=jax.ShapeDtypeStruct((m_z, group, lanes), F32),
        cost_estimate=cost(3 * group * lanes * mat.size, 4 * (n + 3) * slab * group * lanes),
        compiler_params=params(),
        name="conv_z",
    )(*args)


def mul_y(v, hi_ref, lo_ref):
    hi, lo = split(v)
    return dot(hi, hi_ref[...]) + (dot(hi, lo_ref[...]) + dot(lo, hi_ref[...]))


class Blocks:
    def __init__(self, slab, group, size_y):
        self.slab, self.group, self.size_y = slab, group, size_y
        half = size_y // 2
        self.full = pl.BlockSpec((1, slab, group, size_y), lambda s, g: (s, 0, g, 0))
        self.by_group = pl.BlockSpec((slab, group, half), lambda s, g: (s, 0, 0))
        self.a = pl.BlockSpec((slab, group, half), lambda s, g: (0, jnp.where(s == 0, g, 1), 0))
        self.b = pl.BlockSpec((slab, group, half), lambda s, g: (0, jnp.where(s == 0, 0, g), 0))
        self.pieces = [self.by_group, self.by_group, self.a, self.b]
        sds = jax.ShapeDtypeStruct
        self.full_shape = sds((2, slab, 2 * group, size_y), F32)
        self.shapes = [sds((2 * slab, group, half), F32)] * 2 + [sds((slab, 2 * group, half), F32)] * 2
        self.mat = pl.BlockSpec((size_y, size_y), lambda s, g: (0, 0))

    def rows(self, v):
        return v.reshape(self.slab * self.group, v.shape[-1])

    def get(self, e, i, a, b):
        s, g = pl.program_id(0), pl.program_id(1)
        left = jnp.where(g == 0, e[...], i[...])
        right = jnp.where(s == 0, a[...], b[...])
        return jnp.concatenate([self.rows(left), self.rows(right)], axis=1)

    def put(self, v, e, i, a, b):
        s, g = pl.program_id(0), pl.program_id(1)
        half = self.size_y // 2
        left = v[:, :half].reshape(self.slab, self.group, half)
        right = v[:, half:].reshape(self.slab, self.group, half)
        for ref, when, val in ((e, g == 0, left), (i, g == 1, left), (a, s == 0, right), (b, s == 1, right)):

            @pl.when(when)
            def _(ref=ref, val=val):
                ref[...] = val


def first_y(ids, own, received, mat, bl):
    def body(ids_ref, own_ref, got_ref, h_ref, l_ref, obs_ref, *pieces):
        mine = (ids_ref[0] != ids_ref[1]) == (pl.program_id(0) == 0)
        v = jnp.where(mine, own_ref[...], got_ref[...])
        obs_ref[0] = v
        bl.put(mul_y(bl.rows(v), h_ref, l_ref), *pieces)

    src = pl.BlockSpec((bl.slab, bl.group, bl.size_y), lambda s, g: (0, g, 0))
    return pl.pallas_call(
        body,
        grid=(2, 2),
        in_specs=[pl.BlockSpec(memory_space=pltpu.SMEM), src, src, bl.mat, bl.mat],
        out_specs=[bl.full, *bl.pieces],
        out_shape=[bl.full_shape, *bl.shapes],
        compiler_params=params(2),
        name="first_y",
    )(ids, own, received, *mat)


def update_y(estimate, pieces, adj, fwd, bl):
    def body(est_ref, e, i, a, b, ah_ref, al_ref, fh_ref, fl_ref, new_ref, *outs):
        corr = mul_y(bl.get(e, i, a, b), ah_ref, al_ref)
        new = bl.rows(est_ref[0]) * corr
        new_ref[0] = new.reshape(bl.slab, bl.group, bl.size_y)
        bl.put(mul_y(new, fh_ref, fl_ref), *outs)

    return pl.pallas_call(
        body,
        grid=(2, 2),
        in_specs=[bl.full, *bl.pieces] + [bl.mat] * 4,
        out_specs=[bl.full, *bl.pieces],
        out_shape=[bl.full_shape, *bl.shapes],
        compiler_params=params(2),
        name="update_y",
    )(estimate, *pieces, *adj, *fwd)


def last_y(ids, estimate, pieces, adj, bl):
    def body(ids_ref, est_ref, e, i, a, b, ah_ref, al_ref, keep_ref, give_ref):
        corr = mul_y(bl.get(e, i, a, b), ah_ref, al_ref)
        new = (bl.rows(est_ref[0]) * corr).reshape(bl.slab, bl.group, bl.size_y)
        mine = (ids_ref[0] != ids_ref[1]) == (pl.program_id(0) == 0)
        group = pl.ds(pl.multiple_of(pl.program_id(1) * bl.group, bl.group), bl.group)

        @pl.when(mine)
        def _():
            keep_ref[:, group, :] = new

        @pl.when(jnp.logical_not(mine))
        def _():
            give_ref[:, group, :] = new

    whole = pl.BlockSpec((bl.slab, 2 * bl.group, bl.size_y), lambda s, g: (0, 0, 0))
    return pl.pallas_call(
        body,
        grid=(2, 2),
        in_specs=[pl.BlockSpec(memory_space=pltpu.SMEM), bl.full, *bl.pieces] + [bl.mat] * 2,
        out_specs=[whole, whole],
        out_shape=[jax.ShapeDtypeStruct((bl.slab, 2 * bl.group, bl.size_y), F32)] * 2,
        compiler_params=params(2),
        name="last_y",
    )(ids, estimate, *pieces, *adj)


def halves(ids, volume, group):
    slab, _, size_y = volume.shape

    def body(ids_ref, a_ref, b_ref, keep_ref, give_ref):
        keep_ref[...] = a_ref[...]
        give_ref[...] = b_ref[...]

    block = (slab, group, size_y)
    near = pl.BlockSpec(block, lambda g, ids: (0, jnp.where(ids[0] == 0, g, 3 - g), 0))
    far = pl.BlockSpec(block, lambda g, ids: (0, jnp.where(ids[0] == 0, 3 - g, g), 0))
    out = pl.BlockSpec(block, lambda g, ids: (0, g, 0))
    return pl.pallas_call(
        body,
        grid_spec=pltpu.PrefetchScalarGridSpec(num_scalar_prefetch=1, grid=(2,), in_specs=[near, far], out_specs=[out, out]),
        out_shape=[jax.ShapeDtypeStruct((slab, 2 * group, size_y), F32)] * 2,
        compiler_params=params(),
        name="halves",
    )(ids, volume, volume)


def whole_block(ids, own, received, group):
    slab, _, size_y = own.shape

    def body(ids_ref, own_ref, got_ref, out_ref):
        mine = (pl.program_id(0) // 2) == ids_ref[0]
        out_ref[...] = jnp.where(mine, own_ref[...], got_ref[...])

    block = (slab, group, size_y)
    src = pl.BlockSpec(block, lambda g: (0, jnp.minimum(g, 3 - g), 0))
    return pl.pallas_call(
        body,
        grid=(4,),
        in_specs=[pl.BlockSpec(memory_space=pltpu.SMEM), src, src],
        out_specs=pl.BlockSpec(block, lambda g: (0, g, 0)),
        out_shape=jax.ShapeDtypeStruct((slab, 4 * group, size_y), F32),
        compiler_params=params(),
        name="whole_block",
    )(ids, own, received)


def shards(observed, kernel_x, kernel_y, kernel_z):
    n_zg, n_gx = lax.axis_size("zg"), lax.axis_size("gx")
    links = Links(n_zg, n_gx)
    slab, cols, size_y = observed.shape
    group = cols // 4
    assert (kernel_x.shape[0] - 1) // 2 <= group
    assert (kernel_z.shape[0] - 1) // 2 <= slab
    n_pieces = 4 if links.z_odd else 3
    zg = lax.axis_index("zg")
    ids = jnp.stack([zg % 2, (zg // 2) % 2]).astype(jnp.int32)
    bl = Blocks(slab, group, size_y)

    own, give = halves(ids, observed, group)
    received = send(give, links.inner)
    fwd, adj = matrices(ids, kernel_x, kernel_y, kernel_z, slab, group, size_y, n_pieces)

    def x_pass(mat, e, i, over=None, lane=0):
        outer, inner = send(e, links.x), send(i, links.inner)
        return [conv_x(mat, (outer, e, i, inner), s, over, lane) for s in (0, 1)]

    def z_pass(mat, a, b, over=None, lane=0):
        pieces = [a, b, send(a, links.z_even)]
        if links.z_odd:
            pieces.append(send(b, links.z_odd))
        return [conv_z(mat, pieces, g, over, lane) for g in (0, 1)]

    obs, e, i, a, b = first_y(ids, own, received, fwd[1], bl)
    estimate = obs
    for step in range(ITERS):
        left = x_pass(fwd[0], e, i)
        right = z_pass(fwd[2], a, b)
        left = z_pass(fwd[2], *left, over=obs, lane=0)
        right = x_pass(fwd[0], *right, over=obs, lane=1)
        left = x_pass(adj[0], *left)
        right = z_pass(adj[2], *right)
        left = z_pass(adj[2], *left)
        right = x_pass(adj[0], *right)
        if step < ITERS - 1:
            estimate, e, i, a, b = update_y(estimate, (*left, *right), adj[1], fwd[1], bl)
    own, give = last_y(ids, estimate, (*left, *right), adj[1], bl)
    return whole_block(ids, own, send(give, links.inner), group)


def solution(mesh):
    return jax.shard_map(
        shards,
        mesh=mesh,
        in_specs=(P("zg", "gx", None), P(), P(), P()),
        out_specs=P("zg", "gx", None),
        check_vma=False,
    )
```

```python
import functools

import jax
import jax.numpy as jnp
from jax import lax
from jax.experimental import pallas as pl
from jax.experimental.pallas import tpu as pltpu
from jax.sharding import PartitionSpec as P

ITERS = 2
LANES = 128
AXES = ("zg", "gx")
F32 = jnp.float32
BF16 = jnp.bfloat16
VMEM_LIMIT = 40 * 1024 * 1024


def params(n=1):
    return pltpu.CompilerParams(dimension_semantics=("arbitrary",) * n, vmem_limit_bytes=VMEM_LIMIT)


def cost(flops, data):
    return pl.CostEstimate(flops=flops, bytes_accessed=data, transcendentals=0)


def swaps(pairs):
    return [q for a, b in pairs for q in ((a, b), (b, a))]


class Links:
    def __init__(self, n_zg, n_gx):
        chips = n_zg // 2
        dev = lambda z, x: z * n_gx + x
        every = range(n_gx)
        self.inner = swaps((dev(2 * k, x), dev(2 * k + 1, x)) for k in range(chips) for x in every)
        self.x = swaps((dev(2 * k + 1, x), dev(2 * k, (x + 1) % n_gx)) for k in range(chips) for x in every)
        z_pairs = lambda first: swaps(
            (dev(2 * k + c, x), dev(2 * k + 2 + c, x)) for k in range(first, chips - 1, 2) for c in (0, 1) for x in every
        )
        self.z_even = z_pairs(0)
        self.z_odd = z_pairs(1)


def send(v, pairs):
    return lax.ppermute(v, AXES, pairs)


def split(v):
    hi = v.astype(BF16)
    return hi, (v - hi.astype(F32)).astype(BF16)


def dot(a, b):
    return jnp.dot(a, b, preferred_element_type=F32)


def matrices(ids, kernel_x, kernel_y, kernel_z, slab, group, size_y, n_pieces):
    taps_x, taps_y, taps_z = (k.shape[0] for k in (kernel_x, kernel_y, kernel_z))
    half_x, half_y, half_z = ((n - 1) // 2 for n in (taps_x, taps_y, taps_z))
    m_x, k_x = 2 * group, 4 * group
    m_z, k_z = 2 * slab, n_pieces * slab

    def body(ids_ref, x_ref, y_ref, z_ref, fx_ref, ax_ref, fyh_ref, fyl_ref, ayh_ref, ayl_ref, fz_ref, az_ref):
        core, par = ids_ref[0], ids_ref[1]

        def band(ref, n_taps, diff):
            def step(t, carry):
                fwd, adj, total = carry
                tap = ref[t]
                fwd = jnp.where(diff == t, tap, fwd)
                adj = jnp.where(diff == n_taps - 1 - t, tap, adj)
                return fwd, adj, total + tap

            zero = jnp.zeros(diff.shape, F32)
            fwd, adj, total = lax.fori_loop(0, n_taps, step, (zero, zero, jnp.float32(0.0)))
            return fwd / total, adj / total

        def places(shape, dim, size, bases):
            at = lax.broadcasted_iota(jnp.int32, shape, dim)
            place = at
            for n, base in enumerate(bases):
                place = jnp.where(at // size == n, at - n * size + base, place)
            return place

        e, i = group * core, group * (1 - core)
        outer, inner = -group + 3 * group * core + ids_ref[2], 2 * group - 3 * group * core
        rows = places((m_x, k_x), 0, group, (e, i))
        cols = places((m_x, k_x), 1, group, (outer, e, i, inner))
        for ref, mat in zip((fx_ref, ax_ref), band(x_ref, taps_x, cols - rows + half_x)):
            hi, lo = split(mat)
            ref[...] = jnp.concatenate([hi, lo, hi], axis=1)

        a, b = slab * (1 - par), slab * par
        even, odd = 2 * slab - 3 * slab * par, -slab + 3 * slab * par
        rows = places((m_z, k_z), 0, slab, (a, b))
        cols = places((m_z, k_z), 1, slab, (a, b, even, odd)[:n_pieces])
        for ref, mat in zip((fz_ref, az_ref), band(z_ref, taps_z, cols - rows + half_z)):
            hi, lo = split(mat)
            ref[...] = jnp.concatenate([hi, lo], axis=0)

        rows_per = 64
        for r in range(0, size_y, rows_per):
            shape = (rows_per, size_y)
            diff = r + lax.broadcasted_iota(jnp.int32, shape, 0) - lax.broadcasted_iota(jnp.int32, shape, 1) + half_y
            mats = band(y_ref, taps_y, diff)
            for hi_ref, lo_ref, mat in zip((fyh_ref, ayh_ref), (fyl_ref, ayl_ref), mats):
                hi_ref[r : r + rows_per, :], lo_ref[r : r + rows_per, :] = split(mat)

    smem = pl.BlockSpec(memory_space=pltpu.SMEM)
    sds = jax.ShapeDtypeStruct
    out = pl.pallas_call(
        body,
        in_specs=[smem] * 4,
        out_shape=[sds((m_x, 3 * k_x), BF16)] * 2 + [sds((size_y, size_y), BF16)] * 4 + [sds((2 * m_z, k_z), BF16)] * 2,
        compiler_params=pltpu.CompilerParams(vmem_limit_bytes=VMEM_LIMIT),
        name="band_matrices",
    )(ids, kernel_x, kernel_y, kernel_z)
    fx, ax, fyh, fyl, ayh, ayl, fz, az = out
    return (fx, (fyh, fyl), fz), (ax, (ayh, ayl), az)


def conv_x(mat, pieces, s, over=None, lane=0, block=8):
    planes, group, lanes = pieces[0].shape
    slab = planes // 2
    steps = slab // block

    def body(m_ref, *refs):
        out_ref = refs[-1]
        m = m_ref[...]
        for z in range(0, block, 2):
            cols = [jnp.concatenate([r[z + n] for r in refs[:4]], axis=0) for n in (0, 1)]
            hi, lo = split(jnp.concatenate(cols, axis=1))
            res = dot(m, jnp.concatenate([hi, hi, lo], axis=0))
            for n in (0, 1):
                v = res[:, n * lanes : (n + 1) * lanes]
                if over is not None:
                    v = refs[4][0, z + n] / v
                out_ref[z + n] = v

    piece = pl.BlockSpec((block, group, lanes), lambda k: (s * steps + k, 0, 0))
    in_specs = [pl.BlockSpec(mat.shape, lambda k: (0, 0))] + [piece] * 4
    args = [mat, *pieces]
    if over is not None:
        in_specs.append(pl.BlockSpec((1, block, 2 * group, lanes), lambda k: (s, k, 0, lane)))
        args.append(over)
    return pl.pallas_call(
        body,
        grid=(steps,),
        in_specs=in_specs,
        out_specs=pl.BlockSpec((block, 2 * group, lanes), lambda k: (k, 0, 0)),
        out_shape=jax.ShapeDtypeStruct((slab, 2 * group, lanes), F32),
        cost_estimate=cost(2 * slab * lanes * mat.size, 4 * 6 * slab * group * lanes),
        compiler_params=params(),
        name="conv_x",
    )(*args)


def conv_z(mat, pieces, g, over=None, lane=0, block=8):
    slab, width, lanes = pieces[0].shape
    group = width // 2
    steps = group // block
    n = len(pieces)
    m_z = 2 * slab

    def body(m_ref, *refs):
        out = refs[-1].reshape(m_z * block, lanes)
        m = m_ref[...]
        flat = [r.reshape(slab * block, lanes) for r in refs[:n]]
        for x in range(0, block, 2):
            cols = [
                jnp.concatenate([r[pl.ds(x + j, slab, stride=block), :] for r in flat], axis=0) for j in (0, 1)
            ]
            hi, lo = split(jnp.concatenate(cols, axis=1))
            both = dot(m, hi)
            res = both[:m_z] + (both[m_z:] + dot(m[:m_z], lo))
            for j in (0, 1):
                v = res[:, j * lanes : (j + 1) * lanes]
                if over is not None:
                    v = refs[n].reshape(m_z * block, lanes)[pl.ds(x + j, m_z, stride=block), :] / v
                out[pl.ds(x + j, m_z, stride=block), :] = v

    piece = pl.BlockSpec((slab, block, lanes), lambda k: (0, g * steps + k, 0))
    in_specs = [pl.BlockSpec(mat.shape, lambda k: (0, 0))] + [piece] * n
    args = [mat, *pieces]
    if over is not None:
        in_specs.append(pl.BlockSpec((2, slab, block, lanes), lambda k: (0, 0, g * steps + k, lane)))
        args.append(over)
    return pl.pallas_call(
        body,
        grid=(steps,),
        in_specs=in_specs,
        out_specs=pl.BlockSpec((m_z, block, lanes), lambda k: (0, k, 0)),
        out_shape=jax.ShapeDtypeStruct((m_z, group, lanes), F32),
        cost_estimate=cost(3 * group * lanes * mat.size, 4 * (n + 3) * slab * group * lanes),
        compiler_params=params(),
        name="conv_z",
    )(*args)


def mul_y(v, hi_ref, lo_ref):
    hi, lo = split(v)
    return dot(hi, hi_ref[...]) + (dot(hi, lo_ref[...]) + dot(lo, hi_ref[...]))


class Blocks:
    def __init__(self, slab, group, size_y):
        self.slab, self.group, self.size_y = slab, group, size_y
        half = size_y // 2
        self.full = pl.BlockSpec((1, slab, group, size_y), lambda s, g: (s, 0, g, 0))
        self.by_group = pl.BlockSpec((slab, group, half), lambda s, g: (s, 0, 0))
        self.a = pl.BlockSpec((slab, group, half), lambda s, g: (0, jnp.where(s == 0, g, 1), 0))
        self.b = pl.BlockSpec((slab, group, half), lambda s, g: (0, jnp.where(s == 0, 0, g), 0))
        self.pieces = [self.by_group, self.by_group, self.a, self.b]
        sds = jax.ShapeDtypeStruct
        self.full_shape = sds((2, slab, 2 * group, size_y), F32)
        self.shapes = [sds((2 * slab, group, half), F32)] * 2 + [sds((slab, 2 * group, half), F32)] * 2
        self.mat = pl.BlockSpec((size_y, size_y), lambda s, g: (0, 0))

    def rows(self, v):
        return v.reshape(self.slab * self.group, v.shape[-1])

    def get(self, e, i, a, b):
        s, g = pl.program_id(0), pl.program_id(1)
        left = jnp.where(g == 0, e[...], i[...])
        right = jnp.where(s == 0, a[...], b[...])
        return jnp.concatenate([self.rows(left), self.rows(right)], axis=1)

    def put(self, v, e, i, a, b):
        s, g = pl.program_id(0), pl.program_id(1)
        half = self.size_y // 2
        left = v[:, :half].reshape(self.slab, self.group, half)
        right = v[:, half:].reshape(self.slab, self.group, half)
        for ref, when, val in ((e, g == 0, left), (i, g == 1, left), (a, s == 0, right), (b, s == 1, right)):

            @pl.when(when)
            def _(ref=ref, val=val):
                ref[...] = val


def first_y(ids, own, received, mat, bl):
    def body(ids_ref, own_ref, got_ref, h_ref, l_ref, obs_ref, *pieces):
        mine = (ids_ref[0] != ids_ref[1]) == (pl.program_id(0) == 0)
        v = jnp.where(mine, own_ref[...], got_ref[...])
        obs_ref[0] = v
        bl.put(mul_y(bl.rows(v), h_ref, l_ref), *pieces)

    src = pl.BlockSpec((bl.slab, bl.group, bl.size_y), lambda s, g: (0, g, 0))
    return pl.pallas_call(
        body,
        grid=(2, 2),
        in_specs=[pl.BlockSpec(memory_space=pltpu.SMEM), src, src, bl.mat, bl.mat],
        out_specs=[bl.full, *bl.pieces],
        out_shape=[bl.full_shape, *bl.shapes],
        compiler_params=params(2),
        name="first_y",
    )(ids, own, received, *mat)


def update_y(estimate, pieces, adj, fwd, bl):
    def body(est_ref, e, i, a, b, ah_ref, al_ref, fh_ref, fl_ref, new_ref, *outs):
        corr = mul_y(bl.get(e, i, a, b), ah_ref, al_ref)
        new = bl.rows(est_ref[0]) * corr
        new_ref[0] = new.reshape(bl.slab, bl.group, bl.size_y)
        bl.put(mul_y(new, fh_ref, fl_ref), *outs)

    return pl.pallas_call(
        body,
        grid=(2, 2),
        in_specs=[bl.full, *bl.pieces] + [bl.mat] * 4,
        out_specs=[bl.full, *bl.pieces],
        out_shape=[bl.full_shape, *bl.shapes],
        compiler_params=params(2),
        name="update_y",
    )(estimate, *pieces, *adj, *fwd)


def last_y(ids, estimate, pieces, adj, bl):
    def body(ids_ref, est_ref, e, i, a, b, ah_ref, al_ref, keep_ref, give_ref):
        corr = mul_y(bl.get(e, i, a, b), ah_ref, al_ref)
        new = (bl.rows(est_ref[0]) * corr).reshape(bl.slab, bl.group, bl.size_y)
        mine = (ids_ref[0] != ids_ref[1]) == (pl.program_id(0) == 0)
        group = pl.ds(pl.multiple_of(pl.program_id(1) * bl.group, bl.group), bl.group)

        @pl.when(mine)
        def _():
            keep_ref[:, group, :] = new

        @pl.when(jnp.logical_not(mine))
        def _():
            give_ref[:, group, :] = new

    whole = pl.BlockSpec((bl.slab, 2 * bl.group, bl.size_y), lambda s, g: (0, 0, 0))
    return pl.pallas_call(
        body,
        grid=(2, 2),
        in_specs=[pl.BlockSpec(memory_space=pltpu.SMEM), bl.full, *bl.pieces] + [bl.mat] * 2,
        out_specs=[whole, whole],
        out_shape=[jax.ShapeDtypeStruct((bl.slab, 2 * bl.group, bl.size_y), F32)] * 2,
        compiler_params=params(2),
        name="last_y",
    )(ids, estimate, *pieces, *adj)


def halves(ids, volume, group):
    slab, _, size_y = volume.shape

    def body(ids_ref, a_ref, b_ref, keep_ref, give_ref):
        keep_ref[...] = a_ref[...]
        give_ref[...] = b_ref[...]

    block = (slab, group, size_y)
    near = pl.BlockSpec(block, lambda g, ids: (0, jnp.where(ids[0] == 0, g, 3 - g), 0))
    far = pl.BlockSpec(block, lambda g, ids: (0, jnp.where(ids[0] == 0, 3 - g, g), 0))
    out = pl.BlockSpec(block, lambda g, ids: (0, g, 0))
    return pl.pallas_call(
        body,
        grid_spec=pltpu.PrefetchScalarGridSpec(num_scalar_prefetch=1, grid=(2,), in_specs=[near, far], out_specs=[out, out]),
        out_shape=[jax.ShapeDtypeStruct((slab, 2 * group, size_y), F32)] * 2,
        compiler_params=params(),
        name="halves",
    )(ids, volume, volume)


def whole_block(ids, own, received, group):
    slab, _, size_y = own.shape

    def body(ids_ref, own_ref, got_ref, out_ref):
        mine = (pl.program_id(0) // 2) == ids_ref[0]
        out_ref[...] = jnp.where(mine, own_ref[...], got_ref[...])

    block = (slab, group, size_y)
    src = pl.BlockSpec(block, lambda g: (0, jnp.minimum(g, 3 - g), 0))
    return pl.pallas_call(
        body,
        grid=(4,),
        in_specs=[pl.BlockSpec(memory_space=pltpu.SMEM), src, src],
        out_specs=pl.BlockSpec(block, lambda g: (0, g, 0)),
        out_shape=jax.ShapeDtypeStruct((slab, 4 * group, size_y), F32),
        compiler_params=params(),
        name="whole_block",
    )(ids, own, received)


def shards(observed, kernel_x, kernel_y, kernel_z):
    n_zg, n_gx = lax.axis_size("zg"), lax.axis_size("gx")
    links = Links(n_zg, n_gx)
    slab, cols, size_y = observed.shape
    group = cols // 4
    assert (kernel_x.shape[0] - 1) // 2 <= group
    assert (kernel_z.shape[0] - 1) // 2 <= slab
    n_pieces = 4 if links.z_odd else 3
    zg = lax.axis_index("zg")
    gx = lax.axis_index("gx")
    core = zg % 2
    beyond = jnp.where(gx == core * (n_gx - 1), 8 * cols, 0)
    ids = jnp.stack([core, (zg // 2) % 2, beyond]).astype(jnp.int32)
    bl = Blocks(slab, group, size_y)

    own, give = halves(ids, observed, group)
    received = send(give, links.inner)
    fwd, adj = matrices(ids, kernel_x, kernel_y, kernel_z, slab, group, size_y, n_pieces)

    def x_pass(mat, e, i, over=None, lane=0):
        outer, inner = send(e, links.x), send(i, links.inner)
        return [conv_x(mat, (outer, e, i, inner), s, over, lane) for s in (0, 1)]

    def z_pass(mat, a, b, over=None, lane=0):
        pieces = [a, b, send(a, links.z_even)]
        if links.z_odd:
            pieces.append(send(b, links.z_odd))
        return [conv_z(mat, pieces, g, over, lane) for g in (0, 1)]

    obs, e, i, a, b = first_y(ids, own, received, fwd[1], bl)
    estimate = obs
    for step in range(ITERS):
        left = x_pass(fwd[0], e, i)
        right = z_pass(fwd[2], a, b)
        left = z_pass(fwd[2], *left, over=obs, lane=0)
        right = x_pass(fwd[0], *right, over=obs, lane=1)
        left = x_pass(adj[0], *left)
        right = z_pass(adj[2], *right)
        left = z_pass(adj[2], *left)
        right = x_pass(adj[0], *right)
        if step < ITERS - 1:
            estimate, e, i, a, b = update_y(estimate, (*left, *right), adj[1], fwd[1], bl)
    own, give = last_y(ids, estimate, (*left, *right), adj[1], bl)
    return whole_block(ids, own, send(give, links.inner), group)


def solution(mesh):
    return jax.shard_map(
        shards,
        mesh=mesh,
        in_specs=(P("zg", "gx", None), P(), P(), P()),
        out_specs=P("zg", "gx", None),
        check_vma=False,
    )
```

```python
import jax
import jax.numpy as jnp
from jax import lax
from jax.experimental import pallas as pl
from jax.experimental.pallas import tpu as pltpu
from jax.sharding import PartitionSpec as P

ITERS = 2
COST = 30
AXES = ("zg", "gx")
F32 = jnp.float32
BF16 = jnp.bfloat16
VMEM_LIMIT = 24 * 1024 * 1024


def params():
    return pltpu.CompilerParams(vmem_limit_bytes=VMEM_LIMIT)


def cost(flops, data):
    return pl.CostEstimate(flops=int(COST * flops), bytes_accessed=int(COST * data), transcendentals=0)


def shape(*dims, dtype=F32):
    return jax.ShapeDtypeStruct(dims, dtype)


VMEM = pl.BlockSpec(memory_space=pltpu.VMEM)
SMEM = pl.BlockSpec(memory_space=pltpu.SMEM)
HBM = pl.BlockSpec(memory_space=pltpu.HBM)


def swaps(pairs):
    return [q for a, b in pairs for q in ((a, b), (b, a))]


class Links:
    def __init__(self, n_zg, n_gx):
        chips = n_zg // 2
        dev = lambda z, x: z * n_gx + x
        every = range(n_gx)
        self.inner = swaps((dev(2 * k, x), dev(2 * k + 1, x)) for k in range(chips) for x in every)
        self.x = swaps((dev(2 * k + 1, x), dev(2 * k, (x + 1) % n_gx)) for k in range(chips) for x in every)
        z_pairs = lambda first: swaps(
            (dev(2 * k + c, x), dev(2 * k + 2 + c, x)) for k in range(first, chips - 1, 2) for c in (0, 1) for x in every
        )
        self.z_even = z_pairs(0)
        self.z_odd = z_pairs(1)


def send(v, pairs):
    return lax.ppermute(v, AXES, pairs)


def split(v):
    hi = v.astype(BF16)
    return hi, (v - hi.astype(F32)).astype(BF16)


def dot(a, b):
    return jnp.dot(a, b, preferred_element_type=F32)


def band(ref, n_taps, diff):
    def step(t, carry):
        fwd, adj, total = carry
        tap = ref[t]
        return jnp.where(diff == t, tap, fwd), jnp.where(diff == n_taps - 1 - t, tap, adj), total + tap

    zero = jnp.zeros(diff.shape, F32)
    fwd, adj, total = lax.fori_loop(0, n_taps, step, (zero, zero, jnp.float32(0.0)), unroll=True)
    return fwd / total, adj / total


def places(dims, dim, size, bases):
    at = lax.broadcasted_iota(jnp.int32, dims, dim)
    place = at
    for n, base in enumerate(bases):
        place = jnp.where(at // size == n, at - n * size + base, place)
    return place


def matrices_y(kernel_y, size_y, rows_per=64):
    taps = kernel_y.shape[0]

    def body(ref, fh_ref, fl_ref, ah_ref, al_ref):
        dims = (rows_per, size_y)

        @pl.loop(0, size_y // rows_per)
        def _(k):
            at = pl.multiple_of(k * rows_per, rows_per)
            rows = pl.ds(at, rows_per)
            diff = at + lax.broadcasted_iota(jnp.int32, dims, 0) - lax.broadcasted_iota(jnp.int32, dims, 1) + (taps - 1) // 2
            fwd, adj = band(ref, taps, diff)
            fh_ref[rows, :], fl_ref[rows, :] = split(fwd)
            ah_ref[rows, :], al_ref[rows, :] = split(adj)

    out = pl.pallas_call(
        body,
        in_specs=[SMEM],
        out_specs=[VMEM] * 4,
        out_shape=[shape(size_y, size_y, dtype=BF16)] * 4,
        compiler_params=params(),
        name="matrices_y",
    )(kernel_y)
    return out[:2], out[2:]


def matrices_xz(ids, kernel_x, kernel_z, slab, group, n_pieces):
    taps_x, taps_z = kernel_x.shape[0], kernel_z.shape[0]
    m_x, k_x = 2 * group, 4 * group
    m_z, k_z = 2 * slab, n_pieces * slab

    def body(ids_ref, x_ref, z_ref, fx_ref, ax_ref, fz_ref, az_ref):
        core, par = ids_ref[0], ids_ref[1]

        e, i = group * core, group * (1 - core)
        outer, inner = -group + 3 * group * core + ids_ref[2], 2 * group - 3 * group * core
        rows = places((m_x, k_x), 0, group, (e, i))
        cols = places((m_x, k_x), 1, group, (outer, e, i, inner))
        for ref, mat in zip((fx_ref, ax_ref), band(x_ref, taps_x, cols - rows + (taps_x - 1) // 2)):
            hi, lo = split(mat)
            ref[...] = jnp.concatenate([hi, lo, hi], axis=1)

        a, b = slab * (1 - par), slab * par
        even, odd = 2 * slab - 3 * slab * par, -slab + 3 * slab * par
        rows = places((m_z, k_z), 0, slab, (a, b))
        cols = places((m_z, k_z), 1, slab, (a, b, even, odd)[:n_pieces])
        for ref, mat in zip((fz_ref, az_ref), band(z_ref, taps_z, cols - rows + (taps_z - 1) // 2)):
            hi, lo = split(mat)
            ref[...] = jnp.concatenate([hi, lo], axis=0)

    fx, ax, fz, az = pl.pallas_call(
        body,
        in_specs=[SMEM] * 3,
        out_specs=[VMEM] * 4,
        out_shape=[shape(m_x, 3 * k_x, dtype=BF16)] * 2 + [shape(2 * m_z, k_z, dtype=BF16)] * 2,
        compiler_params=params(),
        name="matrices_xz",
    )(ids, kernel_x, kernel_z)
    return (fx, fz), (ax, az)


def conv_x(mat, s, outer, e, i, inner, over):
    slab, group, lanes = e.shape

    def body(m_ref, outer_ref, e_ref, i_ref, inner_ref, *rest):
        out_ref = rest[-1]
        m = m_ref[...]
        at = s * slab
        for z in range(0, slab, 2):
            cols = [
                jnp.concatenate([outer_ref[k], e_ref[k], i_ref[at + k], inner_ref[at + k]], axis=0) for k in (z, z + 1)
            ]
            hi, lo = split(jnp.concatenate(cols, axis=1))
            res = dot(m, jnp.concatenate([hi, hi, lo], axis=0))
            for n in (0, 1):
                v = res[:, n * lanes : (n + 1) * lanes]
                if over is not None:
                    v = rest[0][s, z + n] / v
                out_ref[z + n] = v

    args = [mat, outer, e, i, inner] + ([] if over is None else [over])
    return pl.pallas_call(
        body,
        in_specs=[VMEM] * len(args),
        out_specs=VMEM,
        out_shape=shape(slab, 2 * group, lanes),
        cost_estimate=cost(2 * slab * lanes * mat.size, 4 * 6 * slab * group * lanes),
        compiler_params=params(),
        name="conv_x",
    )(*args)


def conv_z(mat, g, pieces, over):
    slab, width, lanes = pieces[0].shape
    group = width // 2
    n = len(pieces)
    m_z = 2 * slab
    outs = [shape(slab, group, lanes)] * 2 if g == 0 else [shape(m_z, group, lanes)]

    def body(m_ref, *refs):
        m = m_ref[...]
        flat = [r.reshape(slab * width, lanes) for r in refs[:n]]
        out = [r.reshape(r.shape[0] * group, lanes) for r in refs[-len(outs) :]]
        for x in range(0, group, 2):
            cols = [
                jnp.concatenate([r[pl.ds(g * group + x + j, slab, stride=width), :] for r in flat], axis=0) for j in (0, 1)
            ]
            hi, lo = split(jnp.concatenate(cols, axis=1))
            both = dot(m, hi)
            res = both[:m_z] + (both[m_z:] + dot(m[:m_z], lo))
            for j in (0, 1):
                v = res[:, j * lanes : (j + 1) * lanes]
                if over is not None:
                    v = refs[n].reshape(m_z * width, lanes)[pl.ds(g * group + x + j, m_z, stride=width), :] / v
                for r, part in zip(out, jnp.split(v, len(out), axis=0)):
                    r[pl.ds(x + j, part.shape[0], stride=group), :] = part

    args = [mat, *pieces] + ([] if over is None else [over])
    return pl.pallas_call(
        body,
        in_specs=[VMEM] * len(args),
        out_specs=[VMEM] * len(outs),
        out_shape=outs,
        cost_estimate=cost(3 * group * lanes * mat.size, 4 * (n + 3) * slab * group * lanes),
        compiler_params=params(),
        name="conv_z",
    )(*args)


def mul_y(v, hi_ref, lo_ref):
    hi, lo = split(v.reshape(-1, v.shape[-1]))
    res = dot(hi, hi_ref[...]) + (dot(hi, lo_ref[...]) + dot(lo, hi_ref[...]))
    return res.reshape(v.shape)


def take(refs, s, z, block):
    slab = refs[0].shape[0]
    left = jnp.concatenate([refs[s][z : z + block], refs[2][s * slab + z : s * slab + z + block]], axis=1)
    return jnp.concatenate([left, refs[3 + s][z : z + block]], axis=2)


def put(refs, s, z, v):
    slab, group, lanes = refs[0].shape
    block = v.shape[0]
    refs[s][z : z + block] = v[:, :group, :lanes]
    refs[2][s * slab + z : s * slab + z + block] = v[:, group:, :lanes]
    refs[3 + s][z : z + block] = v[:, :, lanes:]


def rows(pair, s, z, block):
    return jnp.concatenate([r[s, z : z + block] for r in pair], axis=2)


def put_rows(pair, s, z, v):
    for r, part in zip(pair, jnp.split(v, 2, axis=2)):
        r[s, z : z + v.shape[0]] = part


def piece_shapes(slab, group, size_y):
    half = size_y // 2
    return [shape(slab, group, half)] * 2 + [shape(2 * slab, group, half)] + [shape(slab, 2 * group, half)] * 2


def own_is_a(ids_ref):
    return ids_ref[0] != ids_ref[1]


def first_y(ids, own, received, mat, block=16):
    slab, width, size_y = own.shape

    def body(ids_ref, own_ref, got_ref, h_ref, l_ref, *refs):
        obs, outs = refs[:2], refs[2:]
        for s in (0, 1):
            mine = own_is_a(ids_ref) == (s == 0)
            for z in range(0, slab, block):
                v = jnp.where(mine, own_ref[z : z + block], got_ref[z : z + block])
                put_rows(obs, s, z, v)
                put(outs, s, z, mul_y(v, h_ref, l_ref))

    out = pl.pallas_call(
        body,
        in_specs=[SMEM] + [VMEM] * 4,
        out_specs=[VMEM] * 7,
        out_shape=[shape(2, slab, width, size_y // 2)] * 2 + piece_shapes(slab, width // 2, size_y),
        compiler_params=params(),
        name="first_y",
    )(ids, own, received, *mat)
    return out[:2], out[2:]


def update_y(estimate, parts, adj, fwd, block=16):
    _, slab, width, half = estimate[0].shape

    def body(*refs):
        est, ins, (ah_ref, al_ref, fh_ref, fl_ref), new_est, outs = refs[:2], refs[2:7], refs[7:11], refs[11:13], refs[13:]
        for s in (0, 1):
            for z in range(0, slab, block):
                new = rows(est, s, z, block) * mul_y(take(ins, s, z, block), ah_ref, al_ref)
                put_rows(new_est, s, z, new)
                put(outs, s, z, mul_y(new, fh_ref, fl_ref))

    out = pl.pallas_call(
        body,
        in_specs=[VMEM] * 11,
        out_specs=[VMEM] * 7,
        out_shape=[shape(2, slab, width, half)] * 2 + piece_shapes(slab, width // 2, 2 * half),
        compiler_params=params(),
        name="update_y",
    )(*estimate, *parts, *adj, *fwd)
    return out[:2], out[2:]


def last_slab(ids, estimate, parts, adj, mine, block=16):
    _, slab, width, half = estimate[0].shape

    def body(ids_ref, *refs):
        est, ins, (ah_ref, al_ref, out_ref) = refs[:2], refs[2:7], refs[7:]
        for s in (0, 1):

            @pl.when(own_is_a(ids_ref) == ((s == 0) == mine))
            def _(s=s):
                for z in range(0, slab, block):
                    out_ref[z : z + block] = rows(est, s, z, block) * mul_y(take(ins, s, z, block), ah_ref, al_ref)

    return pl.pallas_call(
        body,
        in_specs=[SMEM] + [VMEM] * 9,
        out_specs=VMEM,
        out_shape=shape(slab, width, 2 * half),
        compiler_params=params(),
        name="last_slab",
    )(ids, *estimate, *parts, *adj)


def outward(core, g, group):
    at = jnp.where(core == 0, g, 3 - g) * group
    return pl.ds(pl.multiple_of(at, group), group)


def half_of(ids, volume, mine):
    slab, cols, size_y = volume.shape
    group = cols // 4

    def body(ids_ref, src_ref, out_ref, sems):
        core = ids_ref[0] if mine else 1 - ids_ref[0]
        copies = [
            pltpu.make_async_copy(
                src_ref.at[:, outward(core, g, group), :], out_ref.at[:, g * group : (g + 1) * group, :], sems.at[g]
            )
            for g in (0, 1)
        ]
        for c in copies:
            c.start()
        for c in copies:
            c.wait()

    return pl.pallas_call(
        body,
        in_specs=[SMEM, HBM],
        out_specs=VMEM,
        out_shape=shape(slab, 2 * group, size_y),
        scratch_shapes=[pltpu.SemaphoreType.DMA((2,))],
        compiler_params=params(),
        name="half_of",
    )(ids, volume)


def put_half(ids, half, mine, whole=None):
    slab, width, size_y = half.shape
    group = width // 2

    def body(ids_ref, src_ref, *refs):
        out_ref, sems = refs[-2:]
        core = ids_ref[0] if mine else 1 - ids_ref[0]
        copies = [
            pltpu.make_async_copy(
                src_ref.at[:, g * group : (g + 1) * group, :], out_ref.at[:, outward(core, g, group), :], sems.at[g]
            )
            for g in (0, 1)
        ]
        for c in copies:
            c.start()
        for c in copies:
            c.wait()

    args = [ids, half] + ([] if whole is None else [whole])
    return pl.pallas_call(
        body,
        in_specs=[SMEM, VMEM] + ([] if whole is None else [HBM]),
        out_specs=HBM,
        out_shape=shape(slab, 2 * width, size_y),
        scratch_shapes=[pltpu.SemaphoreType.DMA((2,))],
        input_output_aliases={} if whole is None else {2: 0},
        compiler_params=params(),
        name="put_half",
    )(*args)


def shards(observed, kernel_x, kernel_y, kernel_z):
    n_zg, n_gx = lax.axis_size("zg"), lax.axis_size("gx")
    links = Links(n_zg, n_gx)
    slab, cols, size_y = observed.shape
    group = cols // 4
    assert (kernel_x.shape[0] - 1) // 2 <= group
    assert (kernel_z.shape[0] - 1) // 2 <= slab
    n_pieces = 4 if links.z_odd else 3
    zg, gx = lax.axis_index("zg"), lax.axis_index("gx")
    core = zg % 2
    beyond = jnp.where(gx == core * (n_gx - 1), 8 * cols, 0)
    ids = jnp.stack([core, (zg // 2) % 2, beyond]).astype(jnp.int32)

    received = send(half_of(ids, observed, False), links.inner)
    own = half_of(ids, observed, True)
    fwd_y, adj_y = matrices_y(kernel_y, size_y)
    fwd, adj = matrices_xz(ids, kernel_x, kernel_z, slab, group, n_pieces)

    def x_pass(mats, parts, over=None):
        e, i = parts[:2], parts[2]
        outer, inner = [send(v, links.x) for v in e], send(i, links.inner)
        return [conv_x(mats[0], s, outer[s], e[s], i, inner, over) for s in (0, 1)]

    def z_pass(mats, parts, over=None):
        halos = [send(v, pairs) for v, pairs in zip(parts, (links.z_even, links.z_odd)) if pairs]
        return [v for g in (0, 1) for v in conv_z(mats[1], g, [*parts, *halos], over)]

    obs, parts = first_y(ids, own, received, fwd_y)
    estimate = obs
    for step in range(ITERS):
        left, right = parts[:3], parts[3:]
        left, right = x_pass(fwd, left), z_pass(fwd, right)
        left, right = z_pass(fwd, left, obs[0]), x_pass(fwd, right, obs[1])
        left, right = x_pass(adj, left), z_pass(adj, right)
        left, right = z_pass(adj, left), x_pass(adj, right)
        parts = [*left, *right]
        if step < ITERS - 1:
            estimate, parts = update_y(estimate, parts, adj_y, fwd_y)
    received = send(last_slab(ids, estimate, parts, adj_y, False), links.inner)
    whole = put_half(ids, last_slab(ids, estimate, parts, adj_y, True), True)
    return put_half(ids, received, False, whole)


def solution(mesh):
    return jax.shard_map(
        shards,
        mesh=mesh,
        in_specs=(P("zg", "gx", None), P(), P(), P()),
        out_specs=P("zg", "gx", None),
        check_vma=False,
    )
```

```python
import jax
import jax.numpy as jnp
from jax import lax
from jax.experimental import pallas as pl
from jax.experimental.pallas import tpu as pltpu
from jax.sharding import PartitionSpec as P

ITERS = 2
COST_X, COST_Z = 45, 30
AXES = ("zg", "gx")
F32 = jnp.float32
BF16 = jnp.bfloat16
VMEM_LIMIT = 24 * 1024 * 1024


def params():
    return pltpu.CompilerParams(vmem_limit_bytes=VMEM_LIMIT)


def cost(scale, flops, data):
    return pl.CostEstimate(flops=int(scale * flops), bytes_accessed=int(scale * data), transcendentals=0)


def shape(*dims, dtype=F32):
    return jax.ShapeDtypeStruct(dims, dtype)


VMEM = pl.BlockSpec(memory_space=pltpu.VMEM)
SMEM = pl.BlockSpec(memory_space=pltpu.SMEM)
HBM = pl.BlockSpec(memory_space=pltpu.HBM)


def swaps(pairs):
    return [q for a, b in pairs for q in ((a, b), (b, a))]


class Links:
    def __init__(self, n_zg, n_gx):
        chips = n_zg // 2
        dev = lambda z, x: z * n_gx + x
        every = range(n_gx)
        self.inner = swaps((dev(2 * k, x), dev(2 * k + 1, x)) for k in range(chips) for x in every)
        self.x = swaps((dev(2 * k + 1, x), dev(2 * k, (x + 1) % n_gx)) for k in range(chips) for x in every)
        z_pairs = lambda first: swaps(
            (dev(2 * k + c, x), dev(2 * k + 2 + c, x)) for k in range(first, chips - 1, 2) for c in (0, 1) for x in every
        )
        self.z_even = z_pairs(0)
        self.z_odd = z_pairs(1)


def send(v, pairs):
    return lax.ppermute(v, AXES, pairs)


def split(v):
    hi = v.astype(BF16)
    return hi, (v - hi.astype(F32)).astype(BF16)


def dot(a, b):
    return jnp.dot(a, b, preferred_element_type=F32)


def band(ref, n_taps, diff):
    def step(t, carry):
        fwd, adj, total = carry
        tap = ref[t]
        return jnp.where(diff == t, tap, fwd), jnp.where(diff == n_taps - 1 - t, tap, adj), total + tap

    zero = jnp.zeros(diff.shape, F32)
    fwd, adj, total = lax.fori_loop(0, n_taps, step, (zero, zero, jnp.float32(0.0)), unroll=True)
    return fwd / total, adj / total


def places(dims, dim, size, bases):
    at = lax.broadcasted_iota(jnp.int32, dims, dim)
    place = at
    for n, base in enumerate(bases):
        place = jnp.where(at // size == n, at - n * size + base, place)
    return place


def matrices_y(kernel_y, size_y, rows_per=64):
    taps = kernel_y.shape[0]

    def body(ref, fh_ref, fl_ref, ah_ref, al_ref):
        dims = (rows_per, size_y)

        @pl.loop(0, size_y // rows_per)
        def _(k):
            at = pl.multiple_of(k * rows_per, rows_per)
            rows = pl.ds(at, rows_per)
            diff = at + lax.broadcasted_iota(jnp.int32, dims, 0) - lax.broadcasted_iota(jnp.int32, dims, 1) + (taps - 1) // 2
            fwd, adj = band(ref, taps, diff)
            fh_ref[rows, :], fl_ref[rows, :] = split(fwd)
            ah_ref[rows, :], al_ref[rows, :] = split(adj)

    out = pl.pallas_call(
        body,
        in_specs=[SMEM],
        out_specs=[VMEM] * 4,
        out_shape=[shape(size_y, size_y, dtype=BF16)] * 4,
        compiler_params=params(),
        name="matrices_y",
    )(kernel_y)
    return out[:2], out[2:]


def matrices_xz(ids, kernel_x, kernel_z, slab, group, n_pieces):
    taps_x, taps_z = kernel_x.shape[0], kernel_z.shape[0]
    m_x, k_x = 2 * group, 4 * group
    m_z, k_z = 2 * slab, n_pieces * slab

    def body(ids_ref, x_ref, z_ref, fx_ref, ax_ref, fz_ref, az_ref):
        core, par = ids_ref[0], ids_ref[1]

        e, i = group * core, group * (1 - core)
        outer, inner = -group + 3 * group * core + ids_ref[2], 2 * group - 3 * group * core
        rows = places((m_x, k_x), 0, group, (e, i))
        cols = places((m_x, k_x), 1, group, (outer, e, i, inner))
        for ref, mat in zip((fx_ref, ax_ref), band(x_ref, taps_x, cols - rows + (taps_x - 1) // 2)):
            hi, lo = split(mat)
            ref[...] = jnp.concatenate([hi, lo, hi], axis=1)

        a, b = slab * (1 - par), slab * par
        even, odd = 2 * slab - 3 * slab * par, -slab + 3 * slab * par
        rows = places((m_z, k_z), 0, slab, (a, b))
        cols = places((m_z, k_z), 1, slab, (a, b, even, odd)[:n_pieces])
        for ref, mat in zip((fz_ref, az_ref), band(z_ref, taps_z, cols - rows + (taps_z - 1) // 2)):
            hi, lo = split(mat)
            ref[...] = jnp.concatenate([hi, lo], axis=0)

    fx, ax, fz, az = pl.pallas_call(
        body,
        in_specs=[SMEM] * 3,
        out_specs=[VMEM] * 4,
        out_shape=[shape(m_x, 3 * k_x, dtype=BF16)] * 2 + [shape(2 * m_z, k_z, dtype=BF16)] * 2,
        compiler_params=params(),
        name="matrices_xz",
    )(ids, kernel_x, kernel_z)
    return (fx, fz), (ax, az)


def conv_x(mat, s, outer, e, i, inner, over, later=None):
    slab, group, lanes = e.shape
    n_out = 1 if later is None else 2

    def body(m_ref, outer_ref, e_ref, i_ref, inner_ref, *rest):
        out_ref = rest[-n_out]
        if later is not None:
            rest[-1][...] = rest[-n_out - 1][...]
        m = m_ref[...]
        at = s * slab
        for z in range(0, slab, 2):
            cols = [
                jnp.concatenate([outer_ref[k], e_ref[k], i_ref[at + k], inner_ref[at + k]], axis=0) for k in (z, z + 1)
            ]
            hi, lo = split(jnp.concatenate(cols, axis=1))
            res = dot(m, jnp.concatenate([hi, hi, lo], axis=0))
            for n in (0, 1):
                v = res[:, n * lanes : (n + 1) * lanes]
                if over is not None:
                    v = rest[0][s, z + n] / v
                out_ref[z + n] = v

    args = [mat, outer, e, i, inner] + ([] if over is None else [over]) + ([] if later is None else [later])
    return pl.pallas_call(
        body,
        in_specs=[VMEM] * len(args),
        out_specs=[VMEM] * n_out,
        out_shape=[shape(slab, 2 * group, lanes)] + ([] if later is None else [shape(*later.shape)]),
        cost_estimate=cost(COST_X, 2 * slab * lanes * mat.size, 4 * 6 * slab * group * lanes),
        compiler_params=params(),
        name="conv_x",
    )(*args)


def conv_z(mat, g, pieces, over):
    slab, width, lanes = pieces[0].shape
    group = width // 2
    n = len(pieces)
    m_z = 2 * slab
    outs = [shape(slab, group, lanes)] * 2 if g == 0 else [shape(m_z, group, lanes)]

    def body(m_ref, *refs):
        m = m_ref[...]
        flat = [r.reshape(slab * width, lanes) for r in refs[:n]]
        out = [r.reshape(r.shape[0] * group, lanes) for r in refs[-len(outs) :]]
        for x in range(0, group, 2):
            cols = [
                jnp.concatenate([r[pl.ds(g * group + x + j, slab, stride=width), :] for r in flat], axis=0) for j in (0, 1)
            ]
            hi, lo = split(jnp.concatenate(cols, axis=1))
            both = dot(m, hi)
            res = both[:m_z] + (both[m_z:] + dot(m[:m_z], lo))
            for j in (0, 1):
                v = res[:, j * lanes : (j + 1) * lanes]
                if over is not None:
                    v = refs[n].reshape(m_z * width, lanes)[pl.ds(g * group + x + j, m_z, stride=width), :] / v
                for r, part in zip(out, jnp.split(v, len(out), axis=0)):
                    r[pl.ds(x + j, part.shape[0], stride=group), :] = part

    args = [mat, *pieces] + ([] if over is None else [over])
    return pl.pallas_call(
        body,
        in_specs=[VMEM] * len(args),
        out_specs=[VMEM] * len(outs),
        out_shape=outs,
        cost_estimate=cost(COST_Z, 3 * group * lanes * mat.size, 4 * (n + 3) * slab * group * lanes),
        compiler_params=params(),
        name="conv_z",
    )(*args)


def mul_y(v, hi_ref, lo_ref):
    hi, lo = split(v.reshape(-1, v.shape[-1]))
    res = dot(hi, hi_ref[...]) + (dot(hi, lo_ref[...]) + dot(lo, hi_ref[...]))
    return res.reshape(v.shape)


def take(refs, s, z, block):
    slab = refs[0].shape[0]
    left = jnp.concatenate([refs[s][z : z + block], refs[2][s * slab + z : s * slab + z + block]], axis=1)
    return jnp.concatenate([left, refs[3 + s][z : z + block]], axis=2)


def put(refs, s, z, v):
    slab, group, lanes = refs[0].shape
    block = v.shape[0]
    refs[s][z : z + block] = v[:, :group, :lanes]
    refs[2][s * slab + z : s * slab + z + block] = v[:, group:, :lanes]
    refs[3 + s][z : z + block] = v[:, :, lanes:]


def rows(pair, s, z, block):
    return jnp.concatenate([r[s, z : z + block] for r in pair], axis=2)


def put_rows(pair, s, z, v):
    for r, part in zip(pair, jnp.split(v, 2, axis=2)):
        r[s, z : z + v.shape[0]] = part


def piece_shapes(slab, group, size_y):
    half = size_y // 2
    return [shape(slab, group, half)] * 2 + [shape(2 * slab, group, half)] + [shape(slab, 2 * group, half)] * 2


def own_is_a(ids_ref):
    return ids_ref[0] != ids_ref[1]


def first_y(ids, own, received, mat, block=16):
    slab, width, size_y = own.shape

    def body(ids_ref, own_ref, got_ref, h_ref, l_ref, *refs):
        obs, outs = refs[:2], refs[2:]
        for s in (0, 1):
            mine = own_is_a(ids_ref) == (s == 0)
            for z in range(0, slab, block):
                v = jnp.where(mine, own_ref[z : z + block], got_ref[z : z + block])
                put_rows(obs, s, z, v)
                put(outs, s, z, mul_y(v, h_ref, l_ref))

    out = pl.pallas_call(
        body,
        in_specs=[SMEM] + [VMEM] * 4,
        out_specs=[VMEM] * 7,
        out_shape=[shape(2, slab, width, size_y // 2)] * 2 + piece_shapes(slab, width // 2, size_y),
        compiler_params=params(),
        name="first_y",
    )(ids, own, received, *mat)
    return out[:2], out[2:]


def update_y(estimate, parts, adj, fwd, block=16):
    _, slab, width, half = estimate[0].shape

    def body(*refs):
        est, ins, (ah_ref, al_ref, fh_ref, fl_ref), new_est, outs = refs[:2], refs[2:7], refs[7:11], refs[11:13], refs[13:]
        for s in (0, 1):
            for z in range(0, slab, block):
                new = rows(est, s, z, block) * mul_y(take(ins, s, z, block), ah_ref, al_ref)
                put_rows(new_est, s, z, new)
                put(outs, s, z, mul_y(new, fh_ref, fl_ref))

    out = pl.pallas_call(
        body,
        in_specs=[VMEM] * 11,
        out_specs=[VMEM] * 7,
        out_shape=[shape(2, slab, width, half)] * 2 + piece_shapes(slab, width // 2, 2 * half),
        compiler_params=params(),
        name="update_y",
    )(*estimate, *parts, *adj, *fwd)
    return out[:2], out[2:]


def last_slab(ids, estimate, parts, adj, mine, block=16):
    _, slab, width, half = estimate[0].shape

    def body(ids_ref, *refs):
        est, ins, (ah_ref, al_ref, out_ref) = refs[:2], refs[2:7], refs[7:]
        for s in (0, 1):

            @pl.when(own_is_a(ids_ref) == ((s == 0) == mine))
            def _(s=s):
                for z in range(0, slab, block):
                    out_ref[z : z + block] = rows(est, s, z, block) * mul_y(take(ins, s, z, block), ah_ref, al_ref)

    return pl.pallas_call(
        body,
        in_specs=[SMEM] + [VMEM] * 9,
        out_specs=VMEM,
        out_shape=shape(slab, width, 2 * half),
        compiler_params=params(),
        name="last_slab",
    )(ids, *estimate, *parts, *adj)


def outward(core, g, group):
    at = jnp.where(core == 0, g, 3 - g) * group
    return pl.ds(pl.multiple_of(at, group), group)


def half_of(ids, volume, mine):
    slab, cols, size_y = volume.shape
    group = cols // 4

    def body(ids_ref, src_ref, out_ref, sems):
        core = ids_ref[0] if mine else 1 - ids_ref[0]
        copies = [
            pltpu.make_async_copy(
                src_ref.at[:, outward(core, g, group), :], out_ref.at[:, g * group : (g + 1) * group, :], sems.at[g]
            )
            for g in (0, 1)
        ]
        for c in copies:
            c.start()
        for c in copies:
            c.wait()

    return pl.pallas_call(
        body,
        in_specs=[SMEM, HBM],
        out_specs=VMEM,
        out_shape=shape(slab, 2 * group, size_y),
        scratch_shapes=[pltpu.SemaphoreType.DMA((2,))],
        compiler_params=params(),
        name="half_of",
    )(ids, volume)


def put_half(ids, half, mine, whole=None):
    slab, width, size_y = half.shape
    group = width // 2

    def body(ids_ref, src_ref, *refs):
        out_ref, sems = refs[-2:]
        core = ids_ref[0] if mine else 1 - ids_ref[0]
        copies = [
            pltpu.make_async_copy(
                src_ref.at[:, g * group : (g + 1) * group, :], out_ref.at[:, outward(core, g, group), :], sems.at[g]
            )
            for g in (0, 1)
        ]
        for c in copies:
            c.start()
        for c in copies:
            c.wait()

    args = [ids, half] + ([] if whole is None else [whole])
    return pl.pallas_call(
        body,
        in_specs=[SMEM, VMEM] + ([] if whole is None else [HBM]),
        out_specs=HBM,
        out_shape=shape(slab, 2 * width, size_y),
        scratch_shapes=[pltpu.SemaphoreType.DMA((2,))],
        input_output_aliases={} if whole is None else {2: 0},
        compiler_params=params(),
        name="put_half",
    )(*args)


class Chunk:
    def __init__(self, links, mats, over, parts):
        self.links, self.mats, self.over = links, mats, over
        self.parts, self.op, self.out = list(parts), 0, []

    def mat(self, dim):
        return self.mats[self.op // 2][dim]

    def numerator(self):
        return self.over if self.op == 1 else None

    def send_x(self, *which):
        for n in which:
            self.halos[n] = send(self.parts[n], self.links.inner if n == 2 else self.links.x)

    def send_z(self, s, slab):
        pairs = (self.links.z_even, self.links.z_odd)[s]
        if pairs:
            self.halos.append(send(slab, pairs))

    def x(self, s, later=None):
        (e, i), (outer, inner) = ((v[s], v[2]) for v in (self.parts, self.halos))
        out, *late = conv_x(self.mat(0), s, outer, e, i, inner, self.numerator(), later)
        self.out.append(out)
        if s == 1:
            self.turn([])
            self.send_z(0, self.parts[0])
            self.send_z(1, self.parts[1])
        return late[0] if late else None

    def z(self, g):
        self.out += conv_z(self.mat(1), g, [*self.parts, *self.halos], self.numerator())

    def turn(self, halos):
        self.parts, self.out, self.halos = self.out, [], halos
        self.op += 1


def iteration(links, mats, obs, parts):
    left, right = Chunk(links, mats, obs[0], parts[:3]), Chunk(links, mats, obs[1], parts[3:])
    left.halos, right.halos = [None] * 3, []
    left.send_x(2, 0)
    right.send_z(0, parts[3])
    right.send_z(1, parts[4])
    left.send_x(1)
    left.x(0)
    for half in range(4):
        c, other = (right, left) if half % 2 == 0 else (left, right)
        c.z(0)
        c.z(1)
        if half == 3:
            c.turn([])
            other.x(1)
            break
        late = other.x(1, c.out[1])
        c.turn([None] * 3)
        c.parts[1] = late
        c.send_x(0, 2, 1)
        c.x(0)
    return [*left.parts, *right.parts]


def shards(observed, kernel_x, kernel_y, kernel_z):
    n_zg, n_gx = lax.axis_size("zg"), lax.axis_size("gx")
    links = Links(n_zg, n_gx)
    slab, cols, size_y = observed.shape
    group = cols // 4
    assert (kernel_x.shape[0] - 1) // 2 <= group
    assert (kernel_z.shape[0] - 1) // 2 <= slab
    n_pieces = 4 if links.z_odd else 3
    zg, gx = lax.axis_index("zg"), lax.axis_index("gx")
    core = zg % 2
    beyond = jnp.where(gx == core * (n_gx - 1), 8 * cols, 0)
    ids = jnp.stack([core, (zg // 2) % 2, beyond]).astype(jnp.int32)

    received = send(half_of(ids, observed, False), links.inner)
    own = half_of(ids, observed, True)
    fwd_y, adj_y = matrices_y(kernel_y, size_y)
    fwd, adj = matrices_xz(ids, kernel_x, kernel_z, slab, group, n_pieces)

    obs, parts = first_y(ids, own, received, fwd_y)
    estimate = obs
    for step in range(ITERS):
        parts = iteration(links, (fwd, adj), obs, parts)
        if step < ITERS - 1:
            estimate, parts = update_y(estimate, parts, adj_y, fwd_y)
    received = send(last_slab(ids, estimate, parts, adj_y, False), links.inner)
    whole = put_half(ids, last_slab(ids, estimate, parts, adj_y, True), True)
    return put_half(ids, received, False, whole)


def solution(mesh):
    return jax.shard_map(
        shards,
        mesh=mesh,
        in_specs=(P("zg", "gx", None), P(), P(), P()),
        out_specs=P("zg", "gx", None),
        check_vma=False,
    )
```

```python
import jax
import jax.numpy as jnp
from jax import lax
from jax.experimental import pallas as pl
from jax.experimental.pallas import tpu as pltpu
from jax.sharding import PartitionSpec as P

ITERS = 2
COST_X, COST_Z, COST_Y = 45, 30, 0
AXES = ("zg", "gx")
F32 = jnp.float32
BF16 = jnp.bfloat16
VMEM_LIMIT = 24 * 1024 * 1024


def params():
    return pltpu.CompilerParams(vmem_limit_bytes=VMEM_LIMIT)


def cost(scale, flops, data):
    return pl.CostEstimate(flops=int(scale * flops), bytes_accessed=int(scale * data), transcendentals=0)


def shape(*dims, dtype=F32):
    return jax.ShapeDtypeStruct(dims, dtype)


def call(body, args, in_specs, after=None, **options):
    if after is not None:
        n = len(args)
        inner = body
        body = lambda *refs: inner(*refs[:n], *refs[n + 1 :])
        args, in_specs = [*args, after], [*in_specs, pl.BlockSpec(memory_space=pl.ANY)]
    return pl.pallas_call(body, in_specs=in_specs, **options)(*args)


VMEM = pl.BlockSpec(memory_space=pltpu.VMEM)
SMEM = pl.BlockSpec(memory_space=pltpu.SMEM)
HBM = pl.BlockSpec(memory_space=pltpu.HBM)


def swaps(pairs):
    return [q for a, b in pairs for q in ((a, b), (b, a))]


class Links:
    def __init__(self, n_zg, n_gx):
        chips = n_zg // 2
        dev = lambda z, x: z * n_gx + x
        every = range(n_gx)
        self.inner = swaps((dev(2 * k, x), dev(2 * k + 1, x)) for k in range(chips) for x in every)
        self.x = swaps((dev(2 * k + 1, x), dev(2 * k, (x + 1) % n_gx)) for k in range(chips) for x in every)
        z_pairs = lambda first: swaps(
            (dev(2 * k + c, x), dev(2 * k + 2 + c, x)) for k in range(first, chips - 1, 2) for c in (0, 1) for x in every
        )
        self.z_even = z_pairs(0)
        self.z_odd = z_pairs(1)


def send(v, pairs):
    return lax.ppermute(v, AXES, pairs)


def split(v):
    hi = v.astype(BF16)
    return hi, (v - hi.astype(F32)).astype(BF16)


def dot(a, b):
    return jnp.dot(a, b, preferred_element_type=F32)


def band(ref, n_taps, diff):
    def step(t, carry):
        fwd, adj, total = carry
        tap = ref[t]
        return jnp.where(diff == t, tap, fwd), jnp.where(diff == n_taps - 1 - t, tap, adj), total + tap

    zero = jnp.zeros(diff.shape, F32)
    fwd, adj, total = lax.fori_loop(0, n_taps, step, (zero, zero, jnp.float32(0.0)), unroll=True)
    return fwd / total, adj / total


def places(dims, dim, size, bases):
    at = lax.broadcasted_iota(jnp.int32, dims, dim)
    place = at
    for n, base in enumerate(bases):
        place = jnp.where(at // size == n, at - n * size + base, place)
    return place


def matrices_y(kernel_y, size_y):
    taps = kernel_y.shape[0]
    half = (taps - 1) // 2

    def body(ref, fh_ref, fl_ref, ah_ref, al_ref):
        lane = lax.broadcasted_iota(jnp.int32, (1, size_y), 1)
        row, reverse, total = jnp.zeros((1, size_y), F32), jnp.zeros((1, size_y), F32), jnp.float32(0.0)
        for t in range(taps):
            tap = ref[t]
            row, reverse, total = jnp.where(lane == t, tap, row), jnp.where(lane == taps - 1 - t, tap, reverse), total + tap
        dims = (size_y, size_y)
        offset = lax.broadcasted_iota(jnp.int32, dims, 1) - lax.broadcasted_iota(jnp.int32, dims, 0)
        inside = jnp.abs(offset) <= half
        for v, hi_ref, lo_ref in ((reverse, fh_ref, fl_ref), (row, ah_ref, al_ref)):
            mat = pltpu.roll(jnp.broadcast_to(v / total, dims), size_y - half, 1, stride=1, stride_axis=0)
            hi_ref[...], lo_ref[...] = split(jnp.where(inside, mat, 0.0))

    out = pl.pallas_call(
        body,
        in_specs=[SMEM],
        out_specs=[VMEM] * 4,
        out_shape=[shape(size_y, size_y, dtype=BF16)] * 4,
        compiler_params=params(),
        name="matrices_y",
    )(kernel_y)
    return out[:2], out[2:]


def matrices_xz(ids, kernel_x, kernel_z, slab, group, n_pieces):
    taps_x, taps_z = kernel_x.shape[0], kernel_z.shape[0]
    m_x, k_x = 2 * group, 4 * group
    m_z, k_z = 2 * slab, n_pieces * slab

    def body(ids_ref, x_ref, z_ref, fx_ref, ax_ref, fz_ref, az_ref):
        core, par = ids_ref[0], ids_ref[1]

        e, i = group * core, group * (1 - core)
        outer, inner = -group + 3 * group * core + ids_ref[2], 2 * group - 3 * group * core
        rows = places((m_x, k_x), 0, group, (e, i))
        cols = places((m_x, k_x), 1, group, (outer, e, i, inner))
        for ref, mat in zip((fx_ref, ax_ref), band(x_ref, taps_x, cols - rows + (taps_x - 1) // 2)):
            hi, lo = split(mat)
            ref[...] = jnp.concatenate([hi, lo, hi], axis=1)

        a, b = slab * (1 - par), slab * par
        even, odd = 2 * slab - 3 * slab * par, -slab + 3 * slab * par
        rows = places((m_z, k_z), 0, slab, (a, b))
        cols = places((m_z, k_z), 1, slab, (a, b, even, odd)[:n_pieces])
        for ref, mat in zip((fz_ref, az_ref), band(z_ref, taps_z, cols - rows + (taps_z - 1) // 2)):
            hi, lo = split(mat)
            ref[...] = jnp.concatenate([hi, lo], axis=0)

    fx, ax, fz, az = pl.pallas_call(
        body,
        in_specs=[SMEM] * 3,
        out_specs=[VMEM] * 4,
        out_shape=[shape(m_x, 3 * k_x, dtype=BF16)] * 2 + [shape(2 * m_z, k_z, dtype=BF16)] * 2,
        compiler_params=params(),
        name="matrices_xz",
    )(ids, kernel_x, kernel_z)
    return (fx, fz), (ax, az)


def conv_x(mat, s, outer, e, i, inner, over, later=None, after=None):
    slab, group, lanes = e.shape
    n_out = 1 if later is None else 2

    def body(m_ref, outer_ref, e_ref, i_ref, inner_ref, *rest):
        out_ref = rest[-n_out]
        if later is not None:
            rest[-1][...] = rest[-n_out - 1][...]
        m = m_ref[...]
        at = s * slab if i.shape[0] > slab else 0
        for z in range(0, slab, 2):
            cols = [
                jnp.concatenate([outer_ref[k], e_ref[k], i_ref[at + k], inner_ref[at + k]], axis=0) for k in (z, z + 1)
            ]
            hi, lo = split(jnp.concatenate(cols, axis=1))
            res = dot(m, jnp.concatenate([hi, hi, lo], axis=0))
            for n in (0, 1):
                v = res[:, n * lanes : (n + 1) * lanes]
                if over is not None:
                    v = rest[0][z + n] / v
                out_ref[z + n] = v

    args = [mat, outer, e, i, inner] + ([] if over is None else [over]) + ([] if later is None else [later])
    return call(
        body,
        args,
        [VMEM] * len(args),
        after,
        out_specs=[VMEM] * n_out,
        out_shape=[shape(slab, 2 * group, lanes)] + ([] if later is None else [shape(*later.shape)]),
        cost_estimate=cost(COST_X, 2 * slab * lanes * mat.size, 4 * 6 * slab * group * lanes),
        compiler_params=params(),
        name="conv_x",
    )


def conv_z(mat, g, pieces, over):
    slab, width, lanes = pieces[0].shape
    group = width // 2
    n = len(pieces)
    m_z = 2 * slab
    outs = [shape(slab, group, lanes)] * 2 if g == 0 else [shape(m_z, group, lanes)]

    def body(m_ref, *refs):
        m = m_ref[...]
        flat = [r.reshape(slab * width, lanes) for r in refs[:n]]
        out = [r.reshape(r.shape[0] * group, lanes) for r in refs[-len(outs) :]]
        for x in range(0, group, 2):
            cols = [
                jnp.concatenate([r[pl.ds(g * group + x + j, slab, stride=width), :] for r in flat], axis=0) for j in (0, 1)
            ]
            hi, lo = split(jnp.concatenate(cols, axis=1))
            both = dot(m, hi)
            res = both[:m_z] + (both[m_z:] + dot(m[:m_z], lo))
            for j in (0, 1):
                v = res[:, j * lanes : (j + 1) * lanes]
                if over is not None:
                    at = pl.ds(g * group + x + j, slab, stride=width)
                    v = jnp.concatenate([r.reshape(slab * width, lanes)[at, :] for r in refs[n : n + 2]], axis=0) / v
                for r, part in zip(out, jnp.split(v, len(out), axis=0)):
                    r[pl.ds(x + j, part.shape[0], stride=group), :] = part

    args = [mat, *pieces] + list(over or ())
    return pl.pallas_call(
        body,
        in_specs=[VMEM] * len(args),
        out_specs=[VMEM] * len(outs),
        out_shape=outs,
        cost_estimate=cost(COST_Z, 3 * group * lanes * mat.size, 4 * (n + 3) * slab * group * lanes),
        compiler_params=params(),
        name="conv_z",
    )(*args)


def mul_y(v, hi_ref, lo_ref):
    hi, lo = split(v.reshape(-1, v.shape[-1]))
    res = dot(hi, hi_ref[...]) + (dot(hi, lo_ref[...]) + dot(lo, hi_ref[...]))
    return res.reshape(v.shape)


def take(refs, s, z, block):
    e_ref, i_ref, slab_ref = refs
    at = s * e_ref.shape[0] + z
    left = jnp.concatenate([e_ref[z : z + block], i_ref[at : at + block]], axis=1)
    return jnp.concatenate([left, slab_ref[z : z + block]], axis=2)


def put(refs, z, v):
    e_ref, i_ref, slab_ref = refs
    block, group, lanes = v.shape[0], e_ref.shape[1], e_ref.shape[2]
    e_ref[z : z + block] = v[:, :group, :lanes]
    i_ref[z : z + block] = v[:, group:, :lanes]
    slab_ref[z : z + block] = v[:, :, lanes:]


def rows(pair, z, block):
    return jnp.concatenate([r[z : z + block] for r in pair], axis=2)


def put_rows(pair, z, v):
    for r, part in zip(pair, jnp.split(v, 2, axis=2)):
        r[z : z + v.shape[0]] = part


def slab_shapes(slab, width, size_y):
    half = size_y // 2
    return [shape(slab, width, half)] * 2 + [shape(slab, width // 2, half)] * 2 + [shape(slab, width, half)]


def own_is_a(ids_ref):
    return ids_ref[0] != ids_ref[1]


def first_y(ids, s, own, received, mat, block=16):
    slab, width, size_y = own.shape

    def body(ids_ref, own_ref, got_ref, h_ref, l_ref, *refs):
        obs, outs = refs[:2], refs[2:]
        mine = own_is_a(ids_ref) == (s == 0)
        for z in range(0, slab, block):
            v = jnp.where(mine, own_ref[z : z + block], got_ref[z : z + block])
            put_rows(obs, z, v)
            put(outs, z, mul_y(v, h_ref, l_ref))

    out = pl.pallas_call(
        body,
        in_specs=[SMEM] + [VMEM] * 4,
        out_specs=[VMEM] * 5,
        out_shape=slab_shapes(slab, width, size_y),
        cost_estimate=cost(COST_Y, 6 * slab * width * size_y * size_y, 4 * 4 * slab * width * size_y),
        compiler_params=params(),
        name="first_y",
    )(ids, own, received, *mat)
    return out[:2], out[2:]


def update_y(s, estimate, parts, adj, fwd, after=None, block=16):
    slab, width, half = estimate[0].shape

    def body(*refs):
        est, ins, (ah_ref, al_ref, fh_ref, fl_ref), new_est, outs = refs[:2], refs[2:5], refs[5:9], refs[9:11], refs[11:]
        for z in range(0, slab, block):
            new = rows(est, z, block) * mul_y(take(ins, s, z, block), ah_ref, al_ref)
            put_rows(new_est, z, new)
            put(outs, z, mul_y(new, fh_ref, fl_ref))

    out = call(
        body,
        [*estimate, *parts, *adj, *fwd],
        [VMEM] * 9,
        after,
        out_specs=[VMEM] * 5,
        out_shape=slab_shapes(slab, width, 2 * half),
        cost_estimate=cost(COST_Y, 24 * slab * width * half * half, 4 * 8 * slab * width * half),
        compiler_params=params(),
        name="update_y",
    )
    return out[:2], out[2:]


def last_slab(ids, estimate, parts, adj, mine, block=16):
    slab, width, half = estimate[0][0].shape

    def body(ids_ref, *refs):
        est, (e0, e1, i, a, b), (ah_ref, al_ref, out_ref) = (refs[:2], refs[2:4]), refs[4:9], refs[9:]
        ins = ((e0, i, a), (e1, i, b))
        for s in (0, 1):

            @pl.when(own_is_a(ids_ref) == ((s == 0) == mine))
            def _(s=s):
                for z in range(0, slab, block):
                    out_ref[z : z + block] = rows(est[s], z, block) * mul_y(take(ins[s], s, z, block), ah_ref, al_ref)

    return pl.pallas_call(
        body,
        in_specs=[SMEM] + [VMEM] * 11,
        out_specs=VMEM,
        out_shape=shape(slab, width, 2 * half),
        compiler_params=params(),
        name="last_slab",
    )(ids, *estimate[0], *estimate[1], *parts, *adj)


def outward(core, g, group):
    at = jnp.where(core == 0, g, 3 - g) * group
    return pl.ds(pl.multiple_of(at, group), group)


def half_of(ids, volume, mine):
    slab, cols, size_y = volume.shape
    group = cols // 4

    def body(ids_ref, src_ref, out_ref, sems):
        core = ids_ref[0] if mine else 1 - ids_ref[0]
        copies = [
            pltpu.make_async_copy(
                src_ref.at[:, outward(core, g, group), :], out_ref.at[:, g * group : (g + 1) * group, :], sems.at[g]
            )
            for g in (0, 1)
        ]
        for c in copies:
            c.start()
        for c in copies:
            c.wait()

    return pl.pallas_call(
        body,
        in_specs=[SMEM, HBM],
        out_specs=VMEM,
        out_shape=shape(slab, 2 * group, size_y),
        scratch_shapes=[pltpu.SemaphoreType.DMA((2,))],
        compiler_params=params(),
        name="half_of",
    )(ids, volume)


def put_half(ids, half, mine, whole=None):
    slab, width, size_y = half.shape
    group = width // 2

    def body(ids_ref, src_ref, *refs):
        out_ref, sems = refs[-2:]
        core = ids_ref[0] if mine else 1 - ids_ref[0]
        copies = [
            pltpu.make_async_copy(
                src_ref.at[:, g * group : (g + 1) * group, :], out_ref.at[:, outward(core, g, group), :], sems.at[g]
            )
            for g in (0, 1)
        ]
        for c in copies:
            c.start()
        for c in copies:
            c.wait()

    args = [ids, half] + ([] if whole is None else [whole])
    return pl.pallas_call(
        body,
        in_specs=[SMEM, VMEM] + ([] if whole is None else [HBM]),
        out_specs=HBM,
        out_shape=shape(slab, 2 * width, size_y),
        scratch_shapes=[pltpu.SemaphoreType.DMA((2,))],
        input_output_aliases={} if whole is None else {2: 0},
        compiler_params=params(),
        name="put_half",
    )(*args)


class Chunk:
    def __init__(self, links, mats, over, parts):
        self.links, self.mats, self.over = links, mats, over
        self.parts, self.op, self.out = list(parts), 0, []

    def mat(self, dim):
        return self.mats[self.op // 2][dim]

    def numerator(self, s=slice(None)):
        return self.over[s] if self.op == 1 else None

    def send_x(self, *which):
        for n in which:
            if n == 3 and self.parts[3] is self.parts[2]:
                self.halos[3] = self.halos[2]
            else:
                self.halos[n] = send(self.parts[n], self.links.inner if n >= 2 else self.links.x)

    def send_z(self, s, slab):
        pairs = (self.links.z_even, self.links.z_odd)[s]
        if pairs:
            self.halos.append(send(slab, pairs))

    def x(self, s, later=None):
        after = self.out[0] if s == 1 else None
        (e, i), (outer, inner) = ((v[s], v[2 + s]) for v in (self.parts, self.halos))
        out, *late = conv_x(self.mat(0), s, outer, e, i, inner, self.numerator(s), later, after)
        self.out.append(out)
        if s == 1:
            self.turn([])
            if self.op < 4:
                self.send_z(0, self.parts[0])
                self.send_z(1, self.parts[1])
        return late[0] if late else None

    def z(self, g):
        out = conv_z(self.mat(1), g, [*self.parts, *self.halos], self.numerator())
        self.out += out if g == 0 else [out[0], out[0]]

    def turn(self, halos):
        self.parts, self.out, self.halos = self.out, [], halos
        self.op += 1


def iteration(links, mats, obs, parts):
    (e0, i0, a), (e1, i1, b) = parts
    left, right = (Chunk(links, mats, [v[side] for v in obs], p) for side, p in enumerate(([e0, e1, i0, i1], [a, b])))
    left.halos, right.halos = [None] * 4, []
    left.send_x(2, 0)
    right.send_z(0, a)
    right.send_z(1, b)
    left.send_x(3, 1)
    left.x(0)
    for half in range(4):
        c, other = (right, left) if half % 2 == 0 else (left, right)
        c.z(0)
        c.z(1)
        if half == 3:
            c.turn([])
            other.x(1)
            break
        late = other.x(1, c.out[1])
        c.turn([None] * 4)
        c.parts[1] = late
        c.send_x(0, 2, 3, 1)
        c.x(0)
    return [*left.parts[:3], *right.parts]


def shards(observed, kernel_x, kernel_y, kernel_z):
    n_zg, n_gx = lax.axis_size("zg"), lax.axis_size("gx")
    links = Links(n_zg, n_gx)
    slab, cols, size_y = observed.shape
    group = cols // 4
    assert (kernel_x.shape[0] - 1) // 2 <= group
    assert (kernel_z.shape[0] - 1) // 2 <= slab
    n_pieces = 4 if links.z_odd else 3
    zg, gx = lax.axis_index("zg"), lax.axis_index("gx")
    core = zg % 2
    beyond = jnp.where(gx == core * (n_gx - 1), 8 * cols, 0)
    ids = jnp.stack([core, (zg // 2) % 2, beyond]).astype(jnp.int32)

    received = send(half_of(ids, observed, False), links.inner)
    own = half_of(ids, observed, True)
    fwd_y, adj_y = matrices_y(kernel_y, size_y)
    fwd, adj = matrices_xz(ids, kernel_x, kernel_z, slab, group, n_pieces)

    obs, parts = zip(*(first_y(ids, s, own, received, fwd_y) for s in (0, 1)))
    estimate = obs
    for step in range(ITERS):
        e0, e1, i, a, b = iteration(links, (fwd, adj), obs, parts)
        if step < ITERS - 1:
            slabs = ((e0, i, a), (e1, i, b))
            first = update_y(0, estimate[0], slabs[0], adj_y, fwd_y)
            second = update_y(1, estimate[1], slabs[1], adj_y, fwd_y, first[0][0])
            estimate, parts = zip(first, second)
    parts = [e0, e1, i, a, b]
    received = send(last_slab(ids, estimate, parts, adj_y, False), links.inner)
    whole = put_half(ids, last_slab(ids, estimate, parts, adj_y, True), True)
    return put_half(ids, received, False, whole)


def solution(mesh):
    return jax.shard_map(
        shards,
        mesh=mesh,
        in_specs=(P("zg", "gx", None), P(), P(), P()),
        out_specs=P("zg", "gx", None),
        check_vma=False,
    )
```

```python
import jax
import jax.numpy as jnp
from jax import lax
from jax.experimental import pallas as pl
from jax.experimental.pallas import tpu as pltpu
from jax.sharding import PartitionSpec as P

ITERS = 2
COST_X, COST_Z, COST_Y = 45, 30, 0
AXES = ("zg", "gx")
F32 = jnp.float32
BF16 = jnp.bfloat16
VMEM_LIMIT = 24 * 1024 * 1024


def params():
    return pltpu.CompilerParams(vmem_limit_bytes=VMEM_LIMIT)


def cost(scale, flops, data):
    return pl.CostEstimate(flops=int(scale * flops), bytes_accessed=int(scale * data), transcendentals=0)


def shape(*dims, dtype=F32):
    return jax.ShapeDtypeStruct(dims, dtype)


def call(body, args, in_specs, after=None, **options):
    if after is not None:
        n = len(args)
        inner = body
        body = lambda *refs: inner(*refs[:n], *refs[n + 1 :])
        args, in_specs = [*args, after], [*in_specs, pl.BlockSpec(memory_space=pl.ANY)]
    return pl.pallas_call(body, in_specs=in_specs, **options)(*args)


VMEM = pl.BlockSpec(memory_space=pltpu.VMEM)
SMEM = pl.BlockSpec(memory_space=pltpu.SMEM)
HBM = pl.BlockSpec(memory_space=pltpu.HBM)


def swaps(pairs):
    return [q for a, b in pairs for q in ((a, b), (b, a))]


class Links:
    def __init__(self, n_zg, n_gx):
        chips = n_zg // 2
        dev = lambda z, x: z * n_gx + x
        every = range(n_gx)
        self.inner = swaps((dev(2 * k, x), dev(2 * k + 1, x)) for k in range(chips) for x in every)
        self.x = swaps((dev(2 * k + 1, x), dev(2 * k, (x + 1) % n_gx)) for k in range(chips) for x in every)
        z_pairs = lambda first: swaps(
            (dev(2 * k + c, x), dev(2 * k + 2 + c, x)) for k in range(first, chips - 1, 2) for c in (0, 1) for x in every
        )
        self.z_even = z_pairs(0)
        self.z_odd = z_pairs(1)


def send(v, pairs):
    return lax.ppermute(v, AXES, pairs)


def split(v):
    hi = v.astype(BF16)
    return hi, (v - hi.astype(F32)).astype(BF16)


def dot(a, b):
    return jnp.dot(a, b, preferred_element_type=F32)


def band(ref, n_taps, diff):
    def step(t, carry):
        fwd, adj, total = carry
        tap = ref[t]
        return jnp.where(diff == t, tap, fwd), jnp.where(diff == n_taps - 1 - t, tap, adj), total + tap

    zero = jnp.zeros(diff.shape, F32)
    fwd, adj, total = lax.fori_loop(0, n_taps, step, (zero, zero, jnp.float32(0.0)), unroll=True)
    return fwd / total, adj / total


def places(dims, dim, size, bases):
    at = lax.broadcasted_iota(jnp.int32, dims, dim)
    place = at
    for n, base in enumerate(bases):
        place = jnp.where(at // size == n, at - n * size + base, place)
    return place


def matrices_y(kernel_y, size_y):
    taps = kernel_y.shape[0]
    half = (taps - 1) // 2

    def body(ref, fh_ref, fl_ref, ah_ref, al_ref):
        lane = lax.broadcasted_iota(jnp.int32, (1, size_y), 1)
        row, reverse, total = jnp.zeros((1, size_y), F32), jnp.zeros((1, size_y), F32), jnp.float32(0.0)
        for t in range(taps):
            tap = ref[t]
            row, reverse, total = jnp.where(lane == t, tap, row), jnp.where(lane == taps - 1 - t, tap, reverse), total + tap
        dims = (size_y, size_y)
        offset = lax.broadcasted_iota(jnp.int32, dims, 1) - lax.broadcasted_iota(jnp.int32, dims, 0)
        inside = jnp.abs(offset) <= half
        for v, hi_ref, lo_ref in ((reverse, fh_ref, fl_ref), (row, ah_ref, al_ref)):
            mat = pltpu.roll(jnp.broadcast_to(v / total, dims), size_y - half, 1, stride=1, stride_axis=0)
            hi_ref[...], lo_ref[...] = split(jnp.where(inside, mat, 0.0))

    out = pl.pallas_call(
        body,
        in_specs=[SMEM],
        out_specs=[VMEM] * 4,
        out_shape=[shape(size_y, size_y, dtype=BF16)] * 4,
        compiler_params=params(),
        name="matrices_y",
    )(kernel_y)
    return out[:2], out[2:]


def matrices_xz(ids, kernel_x, kernel_z, slab, group, n_pieces):
    taps_x, taps_z = kernel_x.shape[0], kernel_z.shape[0]
    m_x, k_x = 2 * group, 4 * group
    m_z, k_z = 2 * slab, n_pieces * slab

    def body(ids_ref, x_ref, z_ref, fx_ref, ax_ref, fz_ref, az_ref):
        core, par = ids_ref[0], ids_ref[1]

        e, i = group * core, group * (1 - core)
        outer, inner = -group + 3 * group * core + ids_ref[2], 2 * group - 3 * group * core
        rows = places((m_x, k_x), 0, group, (e, i))
        cols = places((m_x, k_x), 1, group, (outer, e, i, inner))
        for ref, mat in zip((fx_ref, ax_ref), band(x_ref, taps_x, cols - rows + (taps_x - 1) // 2)):
            hi, lo = split(mat)
            ref[...] = jnp.concatenate([hi, lo, hi], axis=1)

        a, b = slab * (1 - par), slab * par
        even, odd = 2 * slab - 3 * slab * par, -slab + 3 * slab * par
        rows = places((m_z, k_z), 0, slab, (a, b))
        cols = places((m_z, k_z), 1, slab, (a, b, even, odd)[:n_pieces])
        for ref, mat in zip((fz_ref, az_ref), band(z_ref, taps_z, cols - rows + (taps_z - 1) // 2)):
            hi, lo = split(mat)
            ref[...] = jnp.concatenate([hi, lo], axis=0)

    fx, ax, fz, az = pl.pallas_call(
        body,
        in_specs=[SMEM] * 3,
        out_specs=[VMEM] * 4,
        out_shape=[shape(m_x, 3 * k_x, dtype=BF16)] * 2 + [shape(2 * m_z, k_z, dtype=BF16)] * 2,
        compiler_params=params(),
        name="matrices_xz",
    )(ids, kernel_x, kernel_z)
    return (fx, fz), (ax, az)


def conv_x(mat, s, outer, e, i, inner, over, later=None, after=None):
    slab, group, lanes = e.shape
    n_out = 1 if later is None else 2

    def body(m_ref, outer_ref, e_ref, i_ref, inner_ref, *rest):
        out_ref = rest[-n_out]
        if later is not None:
            rest[-1][...] = rest[-n_out - 1][...]
        m = m_ref[...]
        at = s * slab if i.shape[0] > slab else 0
        for z in range(0, slab, 2):
            cols = [
                jnp.concatenate([outer_ref[k], e_ref[k], i_ref[at + k], inner_ref[at + k]], axis=0) for k in (z, z + 1)
            ]
            hi, lo = split(jnp.concatenate(cols, axis=1))
            res = dot(m, jnp.concatenate([hi, hi, lo], axis=0))
            for n in (0, 1):
                v = res[:, n * lanes : (n + 1) * lanes]
                if over is not None:
                    v = rest[0][z + n] / v
                out_ref[z + n] = v

    args = [mat, outer, e, i, inner] + ([] if over is None else [over]) + ([] if later is None else [later])
    return call(
        body,
        args,
        [VMEM] * len(args),
        after,
        out_specs=[VMEM] * n_out,
        out_shape=[shape(slab, 2 * group, lanes)] + ([] if later is None else [shape(*later.shape)]),
        cost_estimate=cost(COST_X, 2 * slab * lanes * mat.size, 4 * 6 * slab * group * lanes),
        compiler_params=params(),
        name="conv_x",
    )


def conv_z(mat, g, pieces, over):
    slab, width, lanes = pieces[0].shape
    group = width // 2
    n = len(pieces)
    m_z = 2 * slab
    outs = [shape(slab, group, lanes)] * 2 if g == 0 else [shape(m_z, group, lanes)]

    def body(m_ref, *refs):
        m = m_ref[...]
        flat = [r.reshape(slab * width, lanes) for r in refs[:n]]
        out = [r.reshape(r.shape[0] * group, lanes) for r in refs[-len(outs) :]]
        for x in range(0, group, 2):
            cols = [
                jnp.concatenate([r[pl.ds(g * group + x + j, slab, stride=width), :] for r in flat], axis=0) for j in (0, 1)
            ]
            hi, lo = split(jnp.concatenate(cols, axis=1))
            both = dot(m, hi)
            res = both[:m_z] + (both[m_z:] + dot(m[:m_z], lo))
            for j in (0, 1):
                v = res[:, j * lanes : (j + 1) * lanes]
                if over is not None:
                    at = pl.ds(g * group + x + j, slab, stride=width)
                    v = jnp.concatenate([r.reshape(slab * width, lanes)[at, :] for r in refs[n : n + 2]], axis=0) / v
                for r, part in zip(out, jnp.split(v, len(out), axis=0)):
                    r[pl.ds(x + j, part.shape[0], stride=group), :] = part

    args = [mat, *pieces] + list(over or ())
    return pl.pallas_call(
        body,
        in_specs=[VMEM] * len(args),
        out_specs=[VMEM] * len(outs),
        out_shape=outs,
        cost_estimate=cost(COST_Z, 3 * group * lanes * mat.size, 4 * (n + 3) * slab * group * lanes),
        compiler_params=params(),
        name="conv_z",
    )(*args)


def mul_y(v, hi_ref, lo_ref):
    hi, lo = split(v.reshape(-1, v.shape[-1]))
    res = dot(hi, hi_ref[...]) + (dot(hi, lo_ref[...]) + dot(lo, hi_ref[...]))
    return res.reshape(v.shape)


def take(refs, s, z, block):
    e_ref, i_ref, slab_ref = refs
    at = s * e_ref.shape[0] + z
    left = jnp.concatenate([e_ref[z : z + block], i_ref[at : at + block]], axis=1)
    return jnp.concatenate([left, slab_ref[z : z + block]], axis=2)


def put(refs, z, v):
    e_ref, i_ref, slab_ref = refs
    block, group, lanes = v.shape[0], e_ref.shape[1], e_ref.shape[2]
    e_ref[z : z + block] = v[:, :group, :lanes]
    i_ref[z : z + block] = v[:, group:, :lanes]
    slab_ref[z : z + block] = v[:, :, lanes:]


def rows(pair, z, block):
    return jnp.concatenate([r[z : z + block] for r in pair], axis=2)


def put_rows(pair, z, v):
    for r, part in zip(pair, jnp.split(v, 2, axis=2)):
        r[z : z + v.shape[0]] = part


def slab_shapes(slab, width, size_y):
    half = size_y // 2
    return [shape(slab, width, half)] * 2 + [shape(slab, width // 2, half)] * 2 + [shape(slab, width, half)]


def own_is_a(ids_ref):
    return ids_ref[0] != ids_ref[1]


def first_y(ids, s, own, received, mat, block=16):
    slab, width, size_y = own.shape

    def body(ids_ref, own_ref, got_ref, h_ref, l_ref, *refs):
        obs, outs = refs[:2], refs[2:]
        mine = own_is_a(ids_ref) == (s == 0)
        for z in range(0, slab, block):
            v = jnp.where(mine, own_ref[z : z + block], got_ref[z : z + block])
            put_rows(obs, z, v)
            put(outs, z, mul_y(v, h_ref, l_ref))

    out = pl.pallas_call(
        body,
        in_specs=[SMEM] + [VMEM] * 4,
        out_specs=[VMEM] * 5,
        out_shape=slab_shapes(slab, width, size_y),
        cost_estimate=cost(COST_Y, 6 * slab * width * size_y * size_y, 4 * 4 * slab * width * size_y),
        compiler_params=params(),
        name="first_y",
    )(ids, own, received, *mat)
    return out[:2], out[2:]


def update_y(s, estimate, parts, adj, fwd, after=None, block=16):
    slab, width, half = estimate[0].shape

    def body(*refs):
        est, ins, (ah_ref, al_ref, fh_ref, fl_ref), new_est, outs = refs[:2], refs[2:5], refs[5:9], refs[9:11], refs[11:]
        for z in range(0, slab, block):
            new = rows(est, z, block) * mul_y(take(ins, s, z, block), ah_ref, al_ref)
            put_rows(new_est, z, new)
            put(outs, z, mul_y(new, fh_ref, fl_ref))

    out = call(
        body,
        [*estimate, *parts, *adj, *fwd],
        [VMEM] * 9,
        after,
        out_specs=[VMEM] * 5,
        out_shape=slab_shapes(slab, width, 2 * half),
        cost_estimate=cost(COST_Y, 24 * slab * width * half * half, 4 * 8 * slab * width * half),
        compiler_params=params(),
        name="update_y",
    )
    return out[:2], out[2:]


def last_give(ids, estimate, parts, adj, block=16):
    slab, width, half = estimate[0][0].shape

    def body(ids_ref, *refs):
        est, (e0, e1, i, a, b), (ah_ref, al_ref, out_ref) = (refs[:2], refs[2:4]), refs[4:9], refs[9:]
        ins = ((e0, i, a), (e1, i, b))
        for s in (0, 1):

            @pl.when(own_is_a(ids_ref) != (s == 0))
            def _(s=s):
                for z in range(0, slab, block):
                    out_ref[z : z + block] = rows(est[s], z, block) * mul_y(take(ins[s], s, z, block), ah_ref, al_ref)

    return pl.pallas_call(
        body,
        in_specs=[SMEM] + [VMEM] * 11,
        out_specs=VMEM,
        out_shape=shape(slab, width, 2 * half),
        compiler_params=params(),
        name="last_give",
    )(ids, *estimate[0], *estimate[1], *parts, *adj)


def last_own(ids, estimate, parts, adj, block=16):
    slab, width, half = estimate[0][0].shape
    group = width // 2

    def body(ids_ref, *refs):
        est, (e0, e1, i, a, b), (ah_ref, al_ref, out_ref, new_ref, sems) = (refs[:2], refs[2:4]), refs[4:9], refs[9:]
        ins = ((e0, i, a), (e1, i, b))
        copies = [
            [
                pltpu.make_async_copy(
                    new_ref.at[z : z + block, g * group : (g + 1) * group, :],
                    out_ref.at[z : z + block, outward(ids_ref[0], g, group), :],
                    sems.at[z // block, g],
                )
                for g in (0, 1)
            ]
            for z in range(0, slab, block)
        ]
        for s in (0, 1):

            @pl.when(own_is_a(ids_ref) == (s == 0))
            def _(s=s):
                for z in range(0, slab, block):
                    new_ref[z : z + block] = rows(est[s], z, block) * mul_y(take(ins[s], s, z, block), ah_ref, al_ref)
                    for c in copies[z // block]:
                        c.start()

        for pair in copies:
            for c in pair:
                c.wait()

    return pl.pallas_call(
        body,
        in_specs=[SMEM] + [VMEM] * 11,
        out_specs=HBM,
        out_shape=shape(slab, 2 * width, 2 * half),
        scratch_shapes=[pltpu.VMEM((slab, width, 2 * half), F32), pltpu.SemaphoreType.DMA((slab // block, 2))],
        compiler_params=params(),
        name="last_own",
    )(ids, *estimate[0], *estimate[1], *parts, *adj)


def outward(core, g, group):
    at = jnp.where(core == 0, g, 3 - g) * group
    return pl.ds(pl.multiple_of(at, group), group)


def half_of(ids, volume, mine):
    slab, cols, size_y = volume.shape
    group = cols // 4

    def body(ids_ref, src_ref, out_ref, sems):
        core = ids_ref[0] if mine else 1 - ids_ref[0]
        copies = [
            pltpu.make_async_copy(
                src_ref.at[:, outward(core, g, group), :], out_ref.at[:, g * group : (g + 1) * group, :], sems.at[g]
            )
            for g in (0, 1)
        ]
        for c in copies:
            c.start()
        for c in copies:
            c.wait()

    return pl.pallas_call(
        body,
        in_specs=[SMEM, HBM],
        out_specs=VMEM,
        out_shape=shape(slab, 2 * group, size_y),
        scratch_shapes=[pltpu.SemaphoreType.DMA((2,))],
        compiler_params=params(),
        name="half_of",
    )(ids, volume)


def put_half(ids, part, whole):
    _, width, _ = part.shape
    group = width // 2

    def body(ids_ref, src_ref, _, out_ref, sems):
        copies = [
            pltpu.make_async_copy(
                src_ref.at[:, g * group : (g + 1) * group, :],
                out_ref.at[:, outward(1 - ids_ref[0], g, group), :],
                sems.at[g],
            )
            for g in (0, 1)
        ]
        for c in copies:
            c.start()
        for c in copies:
            c.wait()

    return pl.pallas_call(
        body,
        in_specs=[SMEM, VMEM, HBM],
        out_specs=HBM,
        out_shape=shape(*whole.shape),
        scratch_shapes=[pltpu.SemaphoreType.DMA((2,))],
        input_output_aliases={2: 0},
        compiler_params=params(),
        name="put_half",
    )(ids, part, whole)


class Chunk:
    def __init__(self, links, mats, over, parts):
        self.links, self.mats, self.over = links, mats, over
        self.parts, self.op, self.out = list(parts), 0, []

    def mat(self, dim):
        return self.mats[self.op // 2][dim]

    def numerator(self, s=slice(None)):
        return self.over[s] if self.op == 1 else None

    def send_x(self, *which):
        for n in which:
            if n == 3 and self.parts[3] is self.parts[2]:
                self.halos[3] = self.halos[2]
            else:
                self.halos[n] = send(self.parts[n], self.links.inner if n >= 2 else self.links.x)

    def send_z(self, s, slab):
        pairs = (self.links.z_even, self.links.z_odd)[s]
        if pairs:
            self.halos.append(send(slab, pairs))

    def x(self, s, later=None):
        after = self.out[0] if s == 1 else None
        (e, i), (outer, inner) = ((v[s], v[2 + s]) for v in (self.parts, self.halos))
        out, *late = conv_x(self.mat(0), s, outer, e, i, inner, self.numerator(s), later, after)
        self.out.append(out)
        if s == 1:
            self.turn([])
            if self.op < 4:
                self.send_z(0, self.parts[0])
                self.send_z(1, self.parts[1])
        return late[0] if late else None

    def z(self, g):
        out = conv_z(self.mat(1), g, [*self.parts, *self.halos], self.numerator())
        self.out += out if g == 0 else [out[0], out[0]]

    def turn(self, halos):
        self.parts, self.out, self.halos = self.out, [], halos
        self.op += 1


def iteration(links, mats, obs, parts):
    (e0, i0, a), (e1, i1, b) = parts
    left, right = (Chunk(links, mats, [v[side] for v in obs], p) for side, p in enumerate(([e0, e1, i0, i1], [a, b])))
    left.halos, right.halos = [None] * 4, []
    right.send_z(0, a)
    right.send_z(1, b)
    left.send_x(0, 2, 3, 1)
    left.x(0)
    for half in range(4):
        c, other = (right, left) if half % 2 == 0 else (left, right)
        c.z(0)
        c.z(1)
        if half == 3:
            c.turn([])
            other.x(1)
            break
        late = other.x(1, c.out[1])
        c.turn([None] * 4)
        c.parts[1] = late
        c.send_x(0, 2, 3, 1)
        c.x(0)
    return [*left.parts[:3], *right.parts]


def shards(observed, kernel_x, kernel_y, kernel_z):
    n_zg, n_gx = lax.axis_size("zg"), lax.axis_size("gx")
    links = Links(n_zg, n_gx)
    slab, cols, size_y = observed.shape
    group = cols // 4
    assert (kernel_x.shape[0] - 1) // 2 <= group
    assert (kernel_z.shape[0] - 1) // 2 <= slab
    n_pieces = 4 if links.z_odd else 3
    zg, gx = lax.axis_index("zg"), lax.axis_index("gx")
    core = zg % 2
    beyond = jnp.where(gx == core * (n_gx - 1), 8 * cols, 0)
    ids = jnp.stack([core, (zg // 2) % 2, beyond]).astype(jnp.int32)

    received = send(half_of(ids, observed, False), links.inner)
    own = half_of(ids, observed, True)
    fwd_y, adj_y = matrices_y(kernel_y, size_y)
    fwd, adj = matrices_xz(ids, kernel_x, kernel_z, slab, group, n_pieces)

    obs, parts = zip(*(first_y(ids, s, own, received, fwd_y) for s in (0, 1)))
    estimate = obs
    for step in range(ITERS):
        e0, e1, i, a, b = iteration(links, (fwd, adj), obs, parts)
        if step < ITERS - 1:
            slabs = ((e0, i, a), (e1, i, b))
            first = update_y(0, estimate[0], slabs[0], adj_y, fwd_y)
            second = update_y(1, estimate[1], slabs[1], adj_y, fwd_y, first[0][0])
            estimate, parts = zip(first, second)
    parts = [e0, e1, i, a, b]
    received = send(last_give(ids, estimate, parts, adj_y), links.inner)
    return put_half(ids, received, last_own(ids, estimate, parts, adj_y))


def solution(mesh):
    return jax.shard_map(
        shards,
        mesh=mesh,
        in_specs=(P("zg", "gx", None), P(), P(), P()),
        out_specs=P("zg", "gx", None),
        check_vma=False,
    )
```

```python
import jax
import jax.numpy as jnp
from jax import lax
from jax.experimental import pallas as pl
from jax.experimental.pallas import tpu as pltpu
from jax.sharding import PartitionSpec as P

ITERS = 2
COST_X, COST_Z, COST_Y = 45, 30, 0
AXES = ("zg", "gx")
F32 = jnp.float32
BF16 = jnp.bfloat16
VMEM_LIMIT = 24 * 1024 * 1024


def params():
    return pltpu.CompilerParams(vmem_limit_bytes=VMEM_LIMIT)


def cost(scale, flops, data):
    return pl.CostEstimate(flops=int(scale * flops), bytes_accessed=int(scale * data), transcendentals=0)


def shape(*dims, dtype=F32):
    return jax.ShapeDtypeStruct(dims, dtype)


def call(body, args, in_specs, after=None, **options):
    if after is not None:
        n = len(args)
        inner = body
        body = lambda *refs: inner(*refs[:n], *refs[n + 1 :])
        args, in_specs = [*args, after], [*in_specs, pl.BlockSpec(memory_space=pl.ANY)]
    return pl.pallas_call(body, in_specs=in_specs, **options)(*args)


VMEM = pl.BlockSpec(memory_space=pltpu.VMEM)
SMEM = pl.BlockSpec(memory_space=pltpu.SMEM)
HBM = pl.BlockSpec(memory_space=pltpu.HBM)


def swaps(pairs):
    return [q for a, b in pairs for q in ((a, b), (b, a))]


class Links:
    def __init__(self, n_zg, n_gx):
        chips = n_zg // 2
        dev = lambda z, x: z * n_gx + x
        every = range(n_gx)
        self.inner = swaps((dev(2 * k, x), dev(2 * k + 1, x)) for k in range(chips) for x in every)
        self.x = swaps((dev(2 * k + 1, x), dev(2 * k, (x + 1) % n_gx)) for k in range(chips) for x in every)
        z_pairs = lambda first: swaps(
            (dev(2 * k + c, x), dev(2 * k + 2 + c, x)) for k in range(first, chips - 1, 2) for c in (0, 1) for x in every
        )
        self.z_even = z_pairs(0)
        self.z_odd = z_pairs(1)


def send(v, pairs):
    return lax.ppermute(v, AXES, pairs)


def split(v):
    hi = v.astype(BF16)
    return hi, (v - hi.astype(F32)).astype(BF16)


def dot(a, b):
    return jnp.dot(a, b, preferred_element_type=F32)


def band(ref, n_taps, diff):
    def step(t, carry):
        fwd, adj, total = carry
        tap = ref[t]
        return jnp.where(diff == t, tap, fwd), jnp.where(diff == n_taps - 1 - t, tap, adj), total + tap

    zero = jnp.zeros(diff.shape, F32)
    fwd, adj, total = lax.fori_loop(0, n_taps, step, (zero, zero, jnp.float32(0.0)), unroll=True)
    return fwd / total, adj / total


def places(dims, dim, size, bases):
    at = lax.broadcasted_iota(jnp.int32, dims, dim)
    place = at
    for n, base in enumerate(bases):
        place = jnp.where(at // size == n, at - n * size + base, place)
    return place


def matrices_y(kernel_y, size_y):
    taps = kernel_y.shape[0]
    half = (taps - 1) // 2

    def body(ref, fh_ref, fl_ref, ah_ref, al_ref):
        lane = lax.broadcasted_iota(jnp.int32, (1, size_y), 1)
        row, reverse, total = jnp.zeros((1, size_y), F32), jnp.zeros((1, size_y), F32), jnp.float32(0.0)
        for t in range(taps):
            tap = ref[t]
            row, reverse, total = jnp.where(lane == t, tap, row), jnp.where(lane == taps - 1 - t, tap, reverse), total + tap
        dims = (size_y, size_y)
        offset = lax.broadcasted_iota(jnp.int32, dims, 1) - lax.broadcasted_iota(jnp.int32, dims, 0)
        inside = jnp.abs(offset) <= half
        for v, hi_ref, lo_ref in ((reverse, fh_ref, fl_ref), (row, ah_ref, al_ref)):
            mat = pltpu.roll(jnp.broadcast_to(v / total, dims), size_y - half, 1, stride=1, stride_axis=0)
            hi_ref[...], lo_ref[...] = split(jnp.where(inside, mat, 0.0))

    out = pl.pallas_call(
        body,
        in_specs=[SMEM],
        out_specs=[VMEM] * 4,
        out_shape=[shape(size_y, size_y, dtype=BF16)] * 4,
        compiler_params=params(),
        name="matrices_y",
    )(kernel_y)
    return out[:2], out[2:]


def matrices_xz(ids, kernel_x, kernel_z, slab, group, n_pieces):
    taps_x, taps_z = kernel_x.shape[0], kernel_z.shape[0]
    m_x, k_x = 2 * group, 4 * group
    m_z, k_z = 2 * slab, n_pieces * slab

    def body(ids_ref, x_ref, z_ref, fx_ref, ax_ref, fz_ref, az_ref):
        core, par = ids_ref[0], ids_ref[1]

        e, i = group * core, group * (1 - core)
        outer, inner = -group + 3 * group * core + ids_ref[2], 2 * group - 3 * group * core
        rows = places((m_x, k_x), 0, group, (e, i))
        cols = places((m_x, k_x), 1, group, (outer, e, i, inner))
        for ref, mat in zip((fx_ref, ax_ref), band(x_ref, taps_x, cols - rows + (taps_x - 1) // 2)):
            hi, lo = split(mat)
            ref[...] = jnp.concatenate([hi, lo, hi], axis=1)

        a, b = slab * (1 - par), slab * par
        even, odd = 2 * slab - 3 * slab * par, -slab + 3 * slab * par
        rows = places((m_z, k_z), 0, slab, (a, b))
        cols = places((m_z, k_z), 1, slab, (a, b, even, odd)[:n_pieces])
        for ref, mat in zip((fz_ref, az_ref), band(z_ref, taps_z, cols - rows + (taps_z - 1) // 2)):
            hi, lo = split(mat)
            ref[...] = jnp.concatenate([hi, lo], axis=0)

    fx, ax, fz, az = pl.pallas_call(
        body,
        in_specs=[SMEM] * 3,
        out_specs=[VMEM] * 4,
        out_shape=[shape(m_x, 3 * k_x, dtype=BF16)] * 2 + [shape(2 * m_z, k_z, dtype=BF16)] * 2,
        compiler_params=params(),
        name="matrices_xz",
    )(ids, kernel_x, kernel_z)
    return (fx, fz), (ax, az)


def conv_x(mat, s, outer, e, i, inner, over, later=None, after=None):
    slab, group, lanes = e.shape
    n_out = 1 if later is None else 2

    def body(m_ref, outer_ref, e_ref, i_ref, inner_ref, *rest):
        out_ref = rest[-n_out]
        if later is not None:
            rest[-1][...] = rest[-n_out - 1][...]
        m = m_ref[...]
        at = s * slab if i.shape[0] > slab else 0
        for z in range(0, slab, 2):
            cols = [
                jnp.concatenate([outer_ref[k], e_ref[k], i_ref[at + k], inner_ref[at + k]], axis=0) for k in (z, z + 1)
            ]
            hi, lo = split(jnp.concatenate(cols, axis=1))
            res = dot(m, jnp.concatenate([hi, hi, lo], axis=0))
            for n in (0, 1):
                v = res[:, n * lanes : (n + 1) * lanes]
                if over is not None:
                    v = rest[0][z + n] / v
                out_ref[z + n] = v

    args = [mat, outer, e, i, inner] + ([] if over is None else [over]) + ([] if later is None else [later])
    return call(
        body,
        args,
        [VMEM] * len(args),
        after,
        out_specs=[VMEM] * n_out,
        out_shape=[shape(slab, 2 * group, lanes)] + ([] if later is None else [shape(*later.shape)]),
        cost_estimate=cost(COST_X, 2 * slab * lanes * mat.size, 4 * 6 * slab * group * lanes),
        compiler_params=params(),
        name="conv_x",
    )


def conv_z(mat, g, pieces, over):
    slab, width, lanes = pieces[0].shape
    group = width // 2
    n = len(pieces)
    m_z = 2 * slab
    outs = [shape(slab, group, lanes)] * 2 if g == 0 else [shape(m_z, group, lanes)]

    def body(m_ref, *refs):
        m = m_ref[...]
        flat = [r.reshape(slab * width, lanes) for r in refs[:n]]
        out = [r.reshape(r.shape[0] * group, lanes) for r in refs[-len(outs) :]]
        for x in range(0, group, 2):
            cols = [
                jnp.concatenate([r[pl.ds(g * group + x + j, slab, stride=width), :] for r in flat], axis=0) for j in (0, 1)
            ]
            hi, lo = split(jnp.concatenate(cols, axis=1))
            both = dot(m, hi)
            res = both[:m_z] + (both[m_z:] + dot(m[:m_z], lo))
            for j in (0, 1):
                v = res[:, j * lanes : (j + 1) * lanes]
                if over is not None:
                    at = pl.ds(g * group + x + j, slab, stride=width)
                    v = jnp.concatenate([r.reshape(slab * width, lanes)[at, :] for r in refs[n : n + 2]], axis=0) / v
                for r, part in zip(out, jnp.split(v, len(out), axis=0)):
                    r[pl.ds(x + j, part.shape[0], stride=group), :] = part

    args = [mat, *pieces] + list(over or ())
    return pl.pallas_call(
        body,
        in_specs=[VMEM] * len(args),
        out_specs=[VMEM] * len(outs),
        out_shape=outs,
        cost_estimate=cost(COST_Z, 3 * group * lanes * mat.size, 4 * (n + 3) * slab * group * lanes),
        compiler_params=params(),
        name="conv_z",
    )(*args)


def mul_y(v, hi_ref, lo_ref):
    hi, lo = split(v.reshape(-1, v.shape[-1]))
    res = dot(hi, hi_ref[...]) + (dot(hi, lo_ref[...]) + dot(lo, hi_ref[...]))
    return res.reshape(v.shape)


def take(refs, s, z, block):
    e_ref, i_ref, slab_ref = refs
    at = s * e_ref.shape[0] + z
    left = jnp.concatenate([e_ref[z : z + block], i_ref[at : at + block]], axis=1)
    return jnp.concatenate([left, slab_ref[z : z + block]], axis=2)


def put(refs, z, v):
    e_ref, i_ref, slab_ref = refs
    block, group, lanes = v.shape[0], e_ref.shape[1], e_ref.shape[2]
    e_ref[z : z + block] = v[:, :group, :lanes]
    i_ref[z : z + block] = v[:, group:, :lanes]
    slab_ref[z : z + block] = v[:, :, lanes:]


def rows(pair, z, block):
    return jnp.concatenate([r[z : z + block] for r in pair], axis=2)


def put_rows(pair, z, v):
    for r, part in zip(pair, jnp.split(v, 2, axis=2)):
        r[z : z + v.shape[0]] = part


def slab_shapes(slab, width, size_y):
    half = size_y // 2
    return [shape(slab, width, half)] * 2 + [shape(slab, width // 2, half)] * 2 + [shape(slab, width, half)]


def own_is_a(ids_ref):
    return ids_ref[0] != ids_ref[1]


def first_y(ids, s, own, received, mat, block=8):
    slab, width, size_y = own.shape

    def body(ids_ref, own_ref, got_ref, h_ref, l_ref, *refs):
        obs, outs = refs[:2], refs[2:]
        mine = own_is_a(ids_ref) == (s == 0)
        for z in range(0, slab, block):
            v = jnp.where(mine, own_ref[z : z + block], got_ref[z : z + block])
            put_rows(obs, z, v)
            put(outs, z, mul_y(v, h_ref, l_ref))

    out = pl.pallas_call(
        body,
        in_specs=[SMEM] + [VMEM] * 4,
        out_specs=[VMEM] * 5,
        out_shape=slab_shapes(slab, width, size_y),
        cost_estimate=cost(COST_Y, 6 * slab * width * size_y * size_y, 4 * 4 * slab * width * size_y),
        compiler_params=params(),
        name="first_y",
    )(ids, own, received, *mat)
    return out[:2], out[2:]


def update_y(s, estimate, parts, adj, fwd, after=None, block=8):
    slab, width, half = estimate[0].shape

    def body(*refs):
        est, ins, (ah_ref, al_ref, fh_ref, fl_ref), new_est, outs = refs[:2], refs[2:5], refs[5:9], refs[9:11], refs[11:]
        for z in range(0, slab, block):
            new = rows(est, z, block) * mul_y(take(ins, s, z, block), ah_ref, al_ref)
            put_rows(new_est, z, new)
            put(outs, z, mul_y(new, fh_ref, fl_ref))

    out = call(
        body,
        [*estimate, *parts, *adj, *fwd],
        [VMEM] * 9,
        after,
        out_specs=[VMEM] * 5,
        out_shape=slab_shapes(slab, width, 2 * half),
        cost_estimate=cost(COST_Y, 24 * slab * width * half * half, 4 * 8 * slab * width * half),
        compiler_params=params(),
        name="update_y",
    )
    return out[:2], out[2:]


def last_give(ids, estimate, parts, adj, block=8):
    slab, width, half = estimate[0][0].shape

    def body(ids_ref, *refs):
        est, (e0, e1, i, a, b), (ah_ref, al_ref, out_ref) = (refs[:2], refs[2:4]), refs[4:9], refs[9:]
        ins = ((e0, i, a), (e1, i, b))
        for s in (0, 1):

            @pl.when(own_is_a(ids_ref) != (s == 0))
            def _(s=s):
                for z in range(0, slab, block):
                    out_ref[z : z + block] = rows(est[s], z, block) * mul_y(take(ins[s], s, z, block), ah_ref, al_ref)

    return pl.pallas_call(
        body,
        in_specs=[SMEM] + [VMEM] * 11,
        out_specs=VMEM,
        out_shape=shape(slab, width, 2 * half),
        compiler_params=params(),
        name="last_give",
    )(ids, *estimate[0], *estimate[1], *parts, *adj)


def last_own(ids, estimate, parts, adj, block=8):
    slab, width, half = estimate[0][0].shape
    group = width // 2

    def body(ids_ref, *refs):
        est, (e0, e1, i, a, b), (ah_ref, al_ref, out_ref, new_ref, sems) = (refs[:2], refs[2:4]), refs[4:9], refs[9:]
        ins = ((e0, i, a), (e1, i, b))
        copies = [
            [
                pltpu.make_async_copy(
                    new_ref.at[z : z + block, g * group : (g + 1) * group, :],
                    out_ref.at[z : z + block, outward(ids_ref[0], g, group), :],
                    sems.at[z // block, g],
                )
                for g in (0, 1)
            ]
            for z in range(0, slab, block)
        ]
        for s in (0, 1):

            @pl.when(own_is_a(ids_ref) == (s == 0))
            def _(s=s):
                for z in range(0, slab, block):
                    new_ref[z : z + block] = rows(est[s], z, block) * mul_y(take(ins[s], s, z, block), ah_ref, al_ref)
                    for c in copies[z // block]:
                        c.start()

        for pair in copies:
            for c in pair:
                c.wait()

    return pl.pallas_call(
        body,
        in_specs=[SMEM] + [VMEM] * 11,
        out_specs=HBM,
        out_shape=shape(slab, 2 * width, 2 * half),
        scratch_shapes=[pltpu.VMEM((slab, width, 2 * half), F32), pltpu.SemaphoreType.DMA((slab // block, 2))],
        compiler_params=params(),
        name="last_own",
    )(ids, *estimate[0], *estimate[1], *parts, *adj)


def outward(core, g, group):
    at = jnp.where(core == 0, g, 3 - g) * group
    return pl.ds(pl.multiple_of(at, group), group)


def half_of(ids, volume, mine):
    slab, cols, size_y = volume.shape
    group = cols // 4

    def body(ids_ref, src_ref, out_ref, sems):
        core = ids_ref[0] if mine else 1 - ids_ref[0]
        copies = [
            pltpu.make_async_copy(
                src_ref.at[:, outward(core, g, group), :], out_ref.at[:, g * group : (g + 1) * group, :], sems.at[g]
            )
            for g in (0, 1)
        ]
        for c in copies:
            c.start()
        for c in copies:
            c.wait()

    return pl.pallas_call(
        body,
        in_specs=[SMEM, HBM],
        out_specs=VMEM,
        out_shape=shape(slab, 2 * group, size_y),
        scratch_shapes=[pltpu.SemaphoreType.DMA((2,))],
        compiler_params=params(),
        name="half_of",
    )(ids, volume)


def put_half(ids, part, whole):
    _, width, _ = part.shape
    group = width // 2

    def body(ids_ref, src_ref, _, out_ref, sems):
        copies = [
            pltpu.make_async_copy(
                src_ref.at[:, g * group : (g + 1) * group, :],
                out_ref.at[:, outward(1 - ids_ref[0], g, group), :],
                sems.at[g],
            )
            for g in (0, 1)
        ]
        for c in copies:
            c.start()
        for c in copies:
            c.wait()

    return pl.pallas_call(
        body,
        in_specs=[SMEM, VMEM, HBM],
        out_specs=HBM,
        out_shape=shape(*whole.shape),
        scratch_shapes=[pltpu.SemaphoreType.DMA((2,))],
        input_output_aliases={2: 0},
        compiler_params=params(),
        name="put_half",
    )(ids, part, whole)


class Chunk:
    def __init__(self, links, mats, over, parts):
        self.links, self.mats, self.over = links, mats, over
        self.parts, self.op, self.out = list(parts), 0, []

    def mat(self, dim):
        return self.mats[self.op // 2][dim]

    def numerator(self, s=slice(None)):
        return self.over[s] if self.op == 1 else None

    def send_x(self, *which):
        for n in which:
            if n == 3 and self.parts[3] is self.parts[2]:
                self.halos[3] = self.halos[2]
            else:
                self.halos[n] = send(self.parts[n], self.links.inner if n >= 2 else self.links.x)

    def send_z(self, s, slab):
        pairs = (self.links.z_even, self.links.z_odd)[s]
        if pairs:
            self.halos.append(send(slab, pairs))

    def x(self, s, later=None):
        after = self.out[0] if s == 1 else None
        (e, i), (outer, inner) = ((v[s], v[2 + s]) for v in (self.parts, self.halos))
        out, *late = conv_x(self.mat(0), s, outer, e, i, inner, self.numerator(s), later, after)
        self.out.append(out)
        if s == 1:
            self.turn([])
            if self.op < 4:
                self.send_z(0, self.parts[0])
                self.send_z(1, self.parts[1])
        return late[0] if late else None

    def z(self, g):
        out = conv_z(self.mat(1), g, [*self.parts, *self.halos], self.numerator())
        self.out += out if g == 0 else [out[0], out[0]]

    def turn(self, halos):
        self.parts, self.out, self.halos = self.out, [], halos
        self.op += 1


def iteration(links, mats, obs, parts):
    (e0, i0, a), (e1, i1, b) = parts
    left, right = (Chunk(links, mats, [v[side] for v in obs], p) for side, p in enumerate(([e0, e1, i0, i1], [a, b])))
    left.halos, right.halos = [None] * 4, []
    right.send_z(0, a)
    right.send_z(1, b)
    left.send_x(0, 2, 3, 1)
    left.x(0)
    for half in range(4):
        c, other = (right, left) if half % 2 == 0 else (left, right)
        c.z(0)
        c.z(1)
        if half == 3:
            c.turn([])
            other.x(1)
            break
        late = other.x(1, c.out[1])
        c.turn([None] * 4)
        c.parts[1] = late
        c.send_x(0, 2, 3, 1)
        c.x(0)
    return [*left.parts[:3], *right.parts]


def shards(observed, kernel_x, kernel_y, kernel_z):
    n_zg, n_gx = lax.axis_size("zg"), lax.axis_size("gx")
    links = Links(n_zg, n_gx)
    slab, cols, size_y = observed.shape
    group = cols // 4
    assert (kernel_x.shape[0] - 1) // 2 <= group
    assert (kernel_z.shape[0] - 1) // 2 <= slab
    n_pieces = 4 if links.z_odd else 3
    zg, gx = lax.axis_index("zg"), lax.axis_index("gx")
    core = zg % 2
    beyond = jnp.where(gx == core * (n_gx - 1), 8 * cols, 0)
    ids = jnp.stack([core, (zg // 2) % 2, beyond]).astype(jnp.int32)

    received = send(half_of(ids, observed, False), links.inner)
    own = half_of(ids, observed, True)
    fwd_y, adj_y = matrices_y(kernel_y, size_y)
    fwd, adj = matrices_xz(ids, kernel_x, kernel_z, slab, group, n_pieces)

    obs, parts = zip(*(first_y(ids, s, own, received, fwd_y) for s in (0, 1)))
    estimate = obs
    for step in range(ITERS):
        e0, e1, i, a, b = iteration(links, (fwd, adj), obs, parts)
        if step < ITERS - 1:
            slabs = ((e0, i, a), (e1, i, b))
            first = update_y(0, estimate[0], slabs[0], adj_y, fwd_y)
            second = update_y(1, estimate[1], slabs[1], adj_y, fwd_y, first[0][0])
            estimate, parts = zip(first, second)
    parts = [e0, e1, i, a, b]
    received = send(last_give(ids, estimate, parts, adj_y), links.inner)
    return put_half(ids, received, last_own(ids, estimate, parts, adj_y))


def solution(mesh):
    return jax.shard_map(
        shards,
        mesh=mesh,
        in_specs=(P("zg", "gx", None), P(), P(), P()),
        out_specs=P("zg", "gx", None),
        check_vma=False,
    )
```
